128 devices in a mesh: section: 16 (over z_hi, y, core), tp: 8 (over z_lo, x).
Axes of the slice: x: 4, y: 4, z: 4 (z_hi: 2, z_lo: 2; z = z_hi * 2 + z_lo), core: 2. Of those that a mesh axis runs over, the one named last changes fastest.
Arguments:
- arriving: bfloat16 [16, 256, 6144], P('section', None, 'tp'), may hold values from -6 to 6
- cotangent: bfloat16 [16, 256, 6144], P('section', None, 'tp'), may hold values from -6 to 6
- evicted: bfloat16 [16, 2, 256, 6144], P('section', None, None, 'tp'), may hold values from -6 to 6
- ln_gain: float32 [16, 6144], P('section'), may hold values from 0.25 to 1.75
- value_weight: bfloat16 [16, 6144, 6144], P('section', None, 'tp'), may hold values from -0.076546554 to 2.0765466
- out_weight: bfloat16 [16, 6144, 6144], P('section', 'tp'), may hold values from -0.078125 to 0.078125
- fetch_slot: int32 [16], replicated, may hold values from 0 to 1
Outputs:
- forwarded: bfloat16 [16, 256, 6144], P('section', None, 'tp')
- returned: bfloat16 [16, 256, 6144], P('section', None, 'tp')
- gain_grad: float32 [16, 6144], P('section', 'tp')
- fetched: bfloat16 [16, 256, 6144], P('section', None, 'tp')
The draws below stay inside these ranges and needn't reach their ends.
All inputs are finite; a program needn't handle non-finite values.
Results may differ from the reference program's by a relative error of at most 0.017.
Values may be sent and summed in bfloat16 or wider, within the bound.
A program may use at most 128 MiB of HBM per device.

```python
import math
import jax
import jax.numpy as jnp
from jax import lax

D = 6144
HD = 128
LEN = 256
SECTIONS = 16
N_TP = 8


def draw_arriving(key, part):
    key = jax.random.fold_in(key, 1)
    drawn = jnp.clip(jax.random.normal(key, (SECTIONS, LEN, D), jnp.float32), -6.0, 6.0)
    return drawn.astype(jnp.bfloat16)


def draw_evicted(key, part):
    key = jax.random.fold_in(key, 2)
    drawn = jnp.clip(jax.random.normal(key, (SECTIONS * 2, LEN, D), jnp.float32), -6.0, 6.0)
    return drawn.reshape(SECTIONS, 2, LEN, D).astype(jnp.bfloat16)


def draw_value_weight(key, part):
    key = jax.random.fold_in(key, 3)
    drawn = jnp.clip(jax.random.normal(key, (SECTIONS, D, D), jnp.float32), -6.0, 6.0) / math.sqrt(D)
    return drawn.astype(jnp.bfloat16)


def set_ends(entries, key, low, top_value):
    place = [jax.random.randint(jax.random.fold_in(key, axis), (), 0, length) for axis, length in enumerate(entries.shape)]
    main_axis = entries.shape.index(max(entries.shape))
    neighbour = place[:main_axis] + [(place[main_axis] + 1) % entries.shape[main_axis]] + place[main_axis + 1:]
    return entries.at[tuple(place)].set(low).at[tuple(neighbour)].set(top_value)


def block_levels(own_key, dims, pieces, least, high):
    def one(axis_at, blocks):
        heights = jax.random.uniform(jax.random.fold_in(jax.random.fold_in(own_key, 6), axis_at), (blocks,), jnp.float32, least / len(pieces), high / len(pieces))
        return jnp.repeat(jnp.exp(heights), dims[axis_at] // blocks).reshape((-1,) + (1,) * (len(dims) - axis_at - 1))

    level = one(*pieces[0])
    for cut in pieces[1:]:
        level = level * one(*cut)
    return level


def bell_draw(rng, shape, scale, reach, cuts=(), held_as=jnp.bfloat16):
    result = scale * jax.random.normal(rng, shape, jnp.float32)
    if cuts:
        result = result * block_levels(rng, shape, cuts, -0.22, 0.18)
    return jnp.clip(result, -reach, reach).astype(held_as)


def setup_inputs(seed: int = 0) -> dict:
    arg_keys = jax.random.split(jax.random.key(seed), 8)
    return {
        "arriving": draw_arriving(jax.random.fold_in(arg_keys[7], 71), 0),
        "cotangent": bell_draw(arg_keys[1], (SECTIONS, LEN, D), 1.0, 6.0, ((0, 16), (2, 8))),
        "evicted": draw_evicted(jax.random.fold_in(arg_keys[7], 71), 0),
        "ln_gain": jnp.clip(1.0 + 0.15 * jax.random.normal(arg_keys[3], (SECTIONS, D), jnp.float32), 0.25, 1.75),
        "value_weight": draw_value_weight(jax.random.fold_in(arg_keys[7], 71), 0),
        "out_weight": bell_draw(arg_keys[5], (SECTIONS, D, D), D ** -0.5, 0.078125, ((0, 16), (1, 8))),
        "fetch_slot": set_ends(jax.random.randint(arg_keys[6], (SECTIONS,), 0, 2), jax.random.fold_in(arg_keys[6], 1), 0, 1).astype(jnp.int32),
    }


EPS = 1e-05

def layer_norm(row_block, gain_row):
    values = row_block.astype(jnp.float32)
    centre = lax.optimization_barrier(jnp.sum(values, axis=-1, keepdims=True)) / D
    spread = lax.optimization_barrier(jnp.sum(values * values, axis=-1, keepdims=True)) / D - centre * centre
    inv_std = lax.rsqrt(spread + EPS)
    normed = (values - centre) * inv_std
    return (normed, inv_std, (normed * gain_row).astype(jnp.bfloat16))

def head_split(row_block):
    return row_block.reshape(row_block.shape[0], row_block.shape[1] // HD, HD).astype(jnp.float32)

def attend_forward(queries, values):
    q_heads = head_split(queries)
    v_heads = head_split(values)
    length = queries.shape[0]
    scores = jnp.einsum('qhd,khd->hqk', q_heads, v_heads) / math.sqrt(HD)
    causal = jnp.arange(length)[:, None] >= jnp.arange(length)[None, :]
    scores = jnp.where(causal[None], scores, -jnp.inf)
    attn_probs = jax.nn.softmax(scores, axis=-1)
    probs_low = attn_probs.astype(jnp.bfloat16)
    context = jnp.einsum('hqk,khd->qhd', probs_low.astype(jnp.float32), v_heads)
    return (attn_probs, probs_low, context.reshape(length, -1).astype(jnp.bfloat16))

def attend_backward(queries, values, attn_probs, probs_low, grad_context):
    q_heads = head_split(queries)
    v_heads = head_split(values)
    g_heads = head_split(grad_context)
    length = queries.shape[0]
    grad_probs = jnp.einsum('qhd,khd->hqk', g_heads, v_heads)
    grad_scores = attn_probs * (grad_probs - lax.optimization_barrier(jnp.sum(grad_probs * attn_probs, axis=-1, keepdims=True))) / math.sqrt(HD)
    grad_low = lax.optimization_barrier(grad_scores.astype(jnp.bfloat16)).astype(jnp.float32)
    low_probs = probs_low.astype(jnp.float32)
    grad_values = jnp.einsum('hqk,qhd->khd', low_probs, g_heads) + jnp.einsum('hqk,qhd->khd', grad_low, q_heads)
    grad_queries = jnp.einsum('hqk,khd->qhd', grad_low, v_heads)
    return (grad_values.reshape(length, -1).astype(jnp.bfloat16), grad_queries.reshape(length, -1))

def group_total(group_terms):
    rounded = lax.optimization_barrier(group_terms.astype(jnp.bfloat16))
    return lax.optimization_barrier(jnp.sum(rounded.astype(jnp.float32), axis=0))

def reference(arriving, cotangent, evicted, ln_gain, value_weight, out_weight, fetch_slot):
    group_cols = D // N_TP

    def one_section(section_index):
        inputs = arriving[section_index]
        grad_out = cotangent[section_index]
        gain_row = ln_gain[section_index]
        value_mat = value_weight[section_index]
        output_mat = out_weight[section_index]
        partner = (SECTIONS - 1 - section_index).astype(jnp.int32)
        fetched = evicted[partner, fetch_slot[section_index]]
        saved = jnp.where(section_index < SECTIONS // 2, fetched, inputs)
        normed_f, inv_f, scaled_f = layer_norm(inputs, gain_row)
        values_f = jnp.dot(scaled_f, value_mat, preferred_element_type=jnp.float32).astype(jnp.bfloat16)
        probs_f, low_f, context = attend_forward(scaled_f, values_f)
        ctx_groups = context.reshape(LEN, N_TP, group_cols).astype(jnp.float32)
        out_groups = output_mat.reshape(N_TP, group_cols, D).astype(jnp.float32)
        head_mix = group_total(jnp.einsum('lgc,gcd->gld', ctx_groups, out_groups))
        layer_out = (inputs.astype(jnp.float32) + head_mix).astype(jnp.bfloat16)
        normed_b, inv_b, scaled_b = layer_norm(saved, gain_row)
        values_b = jnp.dot(scaled_b, value_mat, preferred_element_type=jnp.float32).astype(jnp.bfloat16)
        probs_b, low_b, unused_context = attend_forward(scaled_b, values_b)
        grad_context = jnp.dot(grad_out, output_mat.T, preferred_element_type=jnp.float32).astype(jnp.bfloat16)
        grad_values, grad_queries = attend_backward(scaled_b, values_b, probs_b, low_b, grad_context)
        value_groups = value_mat.reshape(D, N_TP, group_cols).astype(jnp.float32)
        grad_groups = grad_values.reshape(LEN, N_TP, group_cols).astype(jnp.float32)
        group_terms = jnp.einsum('lgc,dgc->gld', grad_groups, value_groups)
        placed = jnp.einsum('lgc,gh->glhc', grad_queries.reshape(LEN, N_TP, group_cols), jnp.eye(N_TP, dtype=jnp.float32))
        group_terms = group_terms + placed.reshape(N_TP, LEN, D)
        grad_scaled = group_total(group_terms)
        gain_grad = lax.optimization_barrier(jnp.sum(grad_scaled * normed_b, axis=0))
        grad_normed = grad_scaled * gain_row
        first_mean = lax.optimization_barrier(jnp.sum(grad_normed, axis=-1, keepdims=True)) / D
        second_mean = lax.optimization_barrier(jnp.sum(grad_normed * normed_b, axis=-1, keepdims=True)) / D
        grad_inputs = (grad_out.astype(jnp.float32) + inv_b * (grad_normed - first_mean - normed_b * second_mean)).astype(jnp.bfloat16)
        return (layer_out, grad_inputs, gain_grad, fetched)
    outputs_all, grads_all, gain_grads, fetched_all = lax.map(one_section, jnp.arange(SECTIONS, dtype=jnp.int32))
    forwarded = jnp.roll(outputs_all, 1, axis=0)
    returned = jnp.roll(grads_all, -1, axis=0)
    return (forwarded, returned, gain_grads, fetched_all)
```

```python
import math

import jax
import jax.numpy as jnp
from jax import lax
from jax.sharding import PartitionSpec as P

HD = 128


EPS = 1e-05


def shifted(block, axis, distance):
    devices = range(lax.axis_size(axis))
    route = [((i - distance) % len(devices), i) for i in devices]
    return lax.ppermute(block, axis, route)


def layer_norm(row_block, gain_row):
    values = row_block.astype(jnp.float32)
    full_width = row_block.shape[1]
    centre = jnp.sum(values, axis=-1, keepdims=True) / full_width
    spread = jnp.sum(values * values, axis=-1, keepdims=True) / full_width - centre * centre
    inv_std = lax.rsqrt(spread + EPS)
    normed = (values - centre) * inv_std
    return (normed, inv_std, (normed * gain_row).astype(jnp.bfloat16))


def head_view(row_block):
    return row_block.reshape(row_block.shape[0], row_block.shape[1] // HD, HD)


def local_attention(queries, values):
    q_heads = head_view(queries)
    v_heads = head_view(values)
    length = queries.shape[0]
    scores = jnp.einsum(
        "qhd,khd->hqk", q_heads, v_heads, preferred_element_type=jnp.float32
    ) / math.sqrt(HD)
    causal = jnp.arange(length)[:, None] >= jnp.arange(length)[None, :]
    scores = jnp.where(causal[None], scores, -jnp.inf)
    attn_probs = jax.nn.softmax(scores, axis=-1)
    probs_low = attn_probs.astype(jnp.bfloat16)
    context = jnp.einsum("hqk,khd->qhd", probs_low, v_heads, preferred_element_type=jnp.float32)
    return (attn_probs, probs_low, context.reshape(length, -1).astype(jnp.bfloat16))


def local_attention_grad(queries, values, attn_probs, probs_low, grad_context):
    q_heads = head_view(queries)
    v_heads = head_view(values)
    g_heads = head_view(grad_context)
    length = queries.shape[0]
    grad_probs = jnp.einsum("qhd,khd->hqk", g_heads, v_heads, preferred_element_type=jnp.float32)
    grad_scores = (
        attn_probs
        * (grad_probs - jnp.sum(grad_probs * attn_probs, axis=-1, keepdims=True))
        / math.sqrt(HD)
    )
    grad_low = grad_scores.astype(jnp.bfloat16)
    grad_values = jnp.einsum("hqk,qhd->khd", probs_low, g_heads, preferred_element_type=jnp.float32)
    grad_values = grad_values + jnp.einsum(
        "hqk,qhd->khd", grad_low, q_heads, preferred_element_type=jnp.float32
    )
    grad_queries = jnp.einsum("hqk,khd->qhd", grad_low, v_heads, preferred_element_type=jnp.float32)
    return (grad_values.reshape(length, -1).astype(jnp.bfloat16), grad_queries.reshape(length, -1))


def body(arriving, cotangent, evicted, ln_gain, value_weight, out_weight, fetch_slot):
    sections = lax.axis_size("section")
    position = lax.axis_index("section")
    tp_rank = lax.axis_index("tp")
    own_rows = arriving[0]
    own_grad = cotangent[0]
    shard_width = own_rows.shape[1]
    gain_row = ln_gain[0]
    value_local = value_weight[0]
    output_local = out_weight[0]
    head_cols = value_local.shape[1]
    partner = sections - 1 - position
    send_slot = fetch_slot[partner]
    outgoing = lax.dynamic_index_in_dim(evicted[0], send_slot, 0, keepdims=False)
    is_early = position < sections // 2
    col_start = tp_rank * shard_width
    fetched_share = lax.ppermute(
        outgoing, "section", [(i, sections - 1 - i) for i in range(sections)]
    )
    saved_share = jnp.where(is_early, fetched_share, own_rows)
    inputs_full = lax.all_gather(own_rows, "tp", axis=1, tiled=True)
    grad_full = lax.all_gather(own_grad, "tp", axis=1, tiled=True)
    saved_full = lax.all_gather(saved_share, "tp", axis=1, tiled=True)
    full_width = inputs_full.shape[1]
    normed_f, inv_f, scaled_f = layer_norm(inputs_full, gain_row)
    values_f = jnp.dot(scaled_f, value_local, preferred_element_type=jnp.float32).astype(
        jnp.bfloat16
    )
    query_f = lax.dynamic_slice_in_dim(scaled_f, col_start, head_cols, 1)
    probs_f, low_f, context = local_attention(query_f, values_f)
    head_terms = jnp.dot(context, output_local, preferred_element_type=jnp.float32)
    head_mix = lax.psum_scatter(
        head_terms.astype(jnp.bfloat16), "tp", scatter_dimension=1, tiled=True
    ).astype(jnp.float32)
    layer_out = (own_rows.astype(jnp.float32) + head_mix).astype(jnp.bfloat16)
    forwarded = shifted(layer_out, "section", 1)
    normed_b, inv_b, scaled_b = layer_norm(saved_full, gain_row)
    values_b = jnp.dot(scaled_b, value_local, preferred_element_type=jnp.float32).astype(
        jnp.bfloat16
    )
    query_b = lax.dynamic_slice_in_dim(scaled_b, col_start, head_cols, 1)
    probs_b, low_b, unused_context = local_attention(query_b, values_b)
    grad_context = lax.dot_general(
        grad_full, output_local, (((1,), (1,)), ((), ())), preferred_element_type=jnp.float32
    ).astype(jnp.bfloat16)
    grad_values, grad_queries = local_attention_grad(
        query_b, values_b, probs_b, low_b, grad_context
    )
    grad_terms = lax.dot_general(
        grad_values, value_local, (((1,), (1,)), ((), ())), preferred_element_type=jnp.float32
    )
    current = lax.dynamic_slice_in_dim(grad_terms, col_start, head_cols, 1)
    grad_terms = lax.dynamic_update_slice_in_dim(grad_terms, current + grad_queries, col_start, 1)
    grad_own = lax.psum_scatter(
        grad_terms.astype(jnp.bfloat16), "tp", scatter_dimension=1, tiled=True
    ).astype(jnp.float32)
    normed_own = lax.dynamic_slice_in_dim(normed_b, col_start, shard_width, 1)
    gain_own = lax.dynamic_slice_in_dim(gain_row, col_start, shard_width, 0)
    gain_grad = jnp.sum(grad_own * normed_own, axis=0)
    grad_normed = grad_own * gain_own
    sums = jnp.stack(
        [jnp.sum(grad_normed, axis=-1), jnp.sum(grad_normed * normed_own, axis=-1)]
    )
    sums = lax.psum(sums, "tp") / full_width
    first_mean = sums[0][:, None]
    second_mean = sums[1][:, None]
    grad_inputs = (
        own_grad.astype(jnp.float32) + inv_b * (grad_normed - first_mean - normed_own * second_mean)
    ).astype(jnp.bfloat16)
    returned = shifted(grad_inputs, "section", -1)
    return (forwarded[None], returned[None], gain_grad[None], fetched_share[None])


def solution(mesh):
    return jax.shard_map(
        body,
        mesh=mesh,
        in_specs=(
            P("section", None, "tp"),
            P("section", None, "tp"),
            P("section", None, None, "tp"),
            P("section", None),
            P("section", None, "tp"),
            P("section", "tp", None),
            P(),
        ),
        out_specs=(
            P("section", None, "tp"),
            P("section", None, "tp"),
            P("section", "tp"),
            P("section", None, "tp"),
        ),
        check_vma=False,
    )
```

```python
import functools
import math

import jax
import jax.numpy as jnp
from jax import lax
from jax.experimental import pallas as pl
from jax.experimental.pallas import tpu as pltpu
from jax.sharding import PartitionSpec as P

HD = 128
EPS = 1e-05
RING = 4
PEERS = 8
MESH = pl.DeviceIdType.MESH
BF16 = jnp.bfloat16
F32 = jnp.float32
NT = (((1,), (1,)), ((), ()))
NN = (((1,), (0,)), ((), ()))
TN = (((0,), (0,)), ((), ()))


def dot(a, b, dims):
    return lax.dot_general(a, b, dims, preferred_element_type=F32)


def kernel(
    sections,
    arr_ref,
    cot_ref,
    out_ref,
    gain_ref,
    wv_ref,
    wo_ref,
    fwd_ref,
    ret_ref,
    fet_ref,
    gg_ref,
    wv,
    wo,
    cots,
    rows_b,
    rows_f,
    part_g,
    part_h,
    in_g,
    in_h,
    acc,
    grad_ctx,
    val_b,
    val_f,
    grad_val,
    grad_q,
    ctx,
    arr,
    fet,
    normed,
    inv_col,
    stat_out,
    stat_in,
    y_buf,
    dx_buf,
    loc_sem,
    ag_send,
    ag_recv,
    rs_send,
    rs_recv,
    st_send,
    st_recv,
    far_send,
    far_recv,
):
    length, width = arr.shape
    half = length // 2
    heads = width // HD
    full = PEERS * width
    tile = min(256, width)
    section = lax.axis_index("section")
    rank = lax.axis_index("tp")
    x = rank % RING
    z = rank // RING
    early = section < sections // 2

    def at(dx, dz):
        return lax.rem(z + dz, 2) * RING + lax.rem(x + dx + RING, RING)

    def peer(dx, dz):
        return (section, at(dx, dz))

    def remote(src, dst, ssem, rsem, device):
        return pltpu.make_async_remote_copy(
            src_ref=src,
            dst_ref=dst,
            send_sem=ssem,
            recv_sem=rsem,
            device_id=device,
            device_id_type=MESH,
        )

    me = at(0, 0)
    next_section = (lax.rem(section + 1, sections), rank)
    prev_section = (lax.rem(section + sections - 1, sections), rank)
    mirror = (sections - 1 - section, rank)

    load_cot = pltpu.make_async_copy(cot_ref, cots.at[me], loc_sem.at[0])
    load_arr = pltpu.make_async_copy(arr_ref, arr, loc_sem.at[1])
    load_wo = pltpu.make_async_copy(wo_ref, wo, loc_sem.at[2])
    load_wv = pltpu.make_async_copy(wv_ref, wv, loc_sem.at[3])
    load_cot.start()
    load_arr.start()
    load_wo.start()
    load_wv.start()

    barrier = pltpu.get_barrier_semaphore()
    for step in range(1, PEERS):
        pl.semaphore_signal(
            barrier, inc=1, device_id=(section, lax.rem(rank + step, PEERS)), device_id_type=MESH
        )
    for device in (next_section, prev_section, mirror):
        pl.semaphore_signal(barrier, inc=1, device_id=device, device_id_type=MESH)
    pl.semaphore_wait(barrier, PEERS + 2)

    send_far = remote(out_ref, fet, far_send.at[0], far_recv.at[0], mirror)
    send_far.start()

    def gather_edge(buf, g, e, h, landing=False):
        p = 1 - 2 * h
        block, device, landed = (
            ((0, 0), (p, 0), (-p, 0)),
            ((0, 0), (-p, 0), (p, 0)),
            ((0, 0), (0, 1), (0, 1)),
            ((-p, 0), (p, 0), (2, 0)),
            ((2, 0), (0, 1), (2, 1)),
            ((0, 1), (p, 0), (-p, 1)),
            ((0, 1), (-p, 0), (p, 1)),
        )[e]
        rows = buf.at[at(*(landed if landing else block)), pl.ds(h * half, half)]
        return remote(rows, rows, ag_send.at[g, h, e], ag_recv.at[g, h, e], peer(*device))

    def gather_send(buf, g, edges):
        for e in edges:
            for h in range(2):
                gather_edge(buf, g, e, h).start()

    def gather_wait(buf, g, edges):
        for e in edges:
            for h in range(2):
                gather_edge(buf, g, e, h, True).wait_recv()

    def gather_relay(buf, g, e, onward):
        for h in range(2):
            gather_edge(buf, g, e, h, True).wait_recv()
            for o in onward:
                gather_edge(buf, g, o, h).start()

    def gather_drain(buf, g):
        for e in range(7):
            for h in range(2):
                gather_edge(buf, g, e, h).wait_send()

    def consume_cot(blocks, first=False):
        for block in blocks:
            base = pl.multiple_of(block * width, width)

            @pl.loop(0, width // tile)
            def _(n):
                at_n = pl.multiple_of(n * tile, tile)
                term = dot(cots[block], wo[pl.ds(at_n, tile), pl.ds(base, width)], NT)
                if first:
                    acc[:, pl.ds(at_n, tile)] = term
                else:
                    acc[:, pl.ds(at_n, tile)] += term

            first = False

    def consume_rows(buf, blocks, first=False):
        for block in blocks:
            base = pl.multiple_of(block * width, width)

            @pl.loop(0, width // tile)
            def _(n):
                at_n = pl.multiple_of(n * tile, tile)
                term = dot(buf[block], wv[pl.ds(base, width), pl.ds(at_n, tile)], NN)
                if first:
                    acc[:, pl.ds(at_n, tile)] = term
                else:
                    acc[:, pl.ds(at_n, tile)] += term

            first = False

    near = [at(0, 0), at(-1, 0), at(1, 0), at(0, 1)]
    remote_blocks = [at(2, 0), at(-1, 1), at(1, 1), at(2, 1)]

    def row_sums(values, slot):
        total = values[:, 0:HD]
        for c in range(1, width // HD):
            total = total + values[:, c * HD : (c + 1) * HD]
        stat_out[pl.ds(slot, 1), :] = jnp.sum(total.T, axis=0, keepdims=True)

    def stat_copy(turn, step):
        device = (section, lax.rem(rank + step, PEERS))
        return remote(
            stat_out,
            stat_in.at[turn, step - 1],
            st_send.at[turn, step - 1],
            st_recv.at[turn, step - 1],
            device,
        )

    def stats_send(turn):
        for step in range(1, PEERS):
            stat_copy(turn, step).start()

    def stats_total(turn):
        for step in range(1, PEERS):
            stat_copy(turn, step).wait_recv()
        total = stat_out[...]
        for step in range(1, PEERS):
            total = total + stat_in[turn, step - 1]
        return (total / full).T

    load_cot.wait()
    gather_send(cots, 0, (0, 1, 2))
    load_arr.wait()
    stat_out[...] = jnp.zeros_like(stat_out)
    own = arr[...].astype(F32)
    row_sums(own, 0)
    row_sums(own * own, 1)
    gather_relay(cots, 0, 0, (3,))
    gather_relay(cots, 0, 2, (5, 6))
    send_far.wait_recv()
    keep_fet = pltpu.make_async_copy(fet, fet_ref, loc_sem.at[4])
    keep_fet.start()
    saved = jnp.where(early, fet[...].astype(F32), arr[...].astype(F32))
    row_sums(saved, 2)
    row_sums(saved * saved, 3)
    stats_send(0)
    gather_relay(cots, 0, 3, (4,))
    load_wo.wait()
    gather_wait(cots, 0, (1,))
    consume_cot(near, first=True)

    gain = gain_ref[:, pl.ds(pl.multiple_of(rank * width, width), width)]
    means = stats_total(0)
    for turn, buf in ((1, rows_b), (0, rows_f)):
        centre = means[:, 2 * turn : 2 * turn + 1]
        square = means[:, 2 * turn + 1 : 2 * turn + 2]
        inv = lax.rsqrt(square - centre * centre + EPS)
        if turn == 1:
            values = jnp.where(early, fet[...].astype(F32), arr[...].astype(F32))
        else:
            values = arr[...].astype(F32)
        unit = (values - centre) * inv
        buf[me] = (unit * gain).astype(BF16)
        if turn == 1:
            normed[...] = unit
            inv_col[...] = jnp.broadcast_to(inv, inv_col.shape)
            gather_send(rows_b, 1, (0, 1, 2))

    gather_wait(cots, 0, (4, 5, 6))
    consume_cot(remote_blocks)
    grad_ctx[...] = acc[...].astype(BF16)

    gather_relay(rows_b, 1, 0, (3,))
    gather_relay(rows_b, 1, 2, (5, 6))

    @pl.when(early)
    def _():
        gather_send(rows_f, 2, (0, 1, 2))

    gather_relay(rows_b, 1, 3, (4,))
    load_wv.wait()
    gather_wait(rows_b, 1, (1,))
    consume_rows(rows_b, near, first=True)
    gather_wait(rows_b, 1, (4, 5, 6))
    consume_rows(rows_b, remote_blocks)
    val_b[...] = acc[...].astype(BF16)

    @pl.when(early)
    def _():
        gather_relay(rows_f, 2, 0, (3,))
        gather_relay(rows_f, 2, 2, (5, 6))

    row_at = lax.broadcasted_iota(jnp.int32, (length, length), 0)
    col_at = lax.broadcasted_iota(jnp.int32, (length, length), 1)
    scale = 1.0 / math.sqrt(HD)

    def probabilities(q, v):
        scores = dot(q, v, NT) * scale
        scores = jnp.where(col_at <= row_at, scores, -jnp.inf)
        top = jnp.max(scores, axis=-1, keepdims=True)
        e = jnp.exp(scores - top)
        return e / jnp.sum(e, axis=-1, keepdims=True)

    @pl.loop(0, heads)
    def _(head):
        cols = pl.ds(pl.multiple_of(head * HD, HD), HD)
        q = rows_b[me, :, cols]
        v = val_b[:, cols]
        g = grad_ctx[:, cols]
        probs = probabilities(q, v)
        low = probs.astype(BF16)
        grad_probs = dot(g, v, NT)
        inner = jnp.sum(grad_probs * probs, axis=-1, keepdims=True)
        grad_low = (probs * (grad_probs - inner) * scale).astype(BF16)
        grad_val[:, cols] = (dot(low, g, TN) + dot(grad_low, q, TN)).astype(BF16)
        grad_q[:, cols] = dot(grad_low, v, NN)

    def reduce_edge(part, inbox, r, e, h):
        p = 1 - 2 * h
        block, device = (
            ((2, 1), (0, 1)),
            ((-p, 1), (-p, 0)),
            ((p, 1), (p, 0)),
            ((p, 0), (p, 0)),
            ((2, 0), (-p, 0)),
            ((-p, 0), (-p, 0)),
            ((0, 1), (0, 1)),
        )[e]
        mine = part.at[at(*block), pl.ds(h * half, half)]
        return remote(
            mine, inbox.at[h, e], rs_send.at[r, h, e], rs_recv.at[r, h, e], peer(*device)
        ), at(*block)

    def reduce_send(part, inbox, r, e, h):
        reduce_edge(part, inbox, r, e, h)[0].start()

    def reduce_relay(part, inbox, r, e, sources):
        for h in range(2):
            copy, block = reduce_edge(part, inbox, r, e, h)
            at_h = pl.ds(h * half, half)
            total = part[block, at_h].astype(F32)
            for s in sources:
                reduce_edge(part, inbox, r, s, h)[0].wait_recv()
                total = total + inbox[h, s].astype(F32)
            part[block, at_h] = total.astype(BF16)
            copy.start()

    def reduce_final(part, inbox, r, h):
        total = part[me, pl.ds(h * half, half)].astype(F32)
        for s in (3, 6, 5):
            reduce_edge(part, inbox, r, s, h)[0].wait_recv()
            total = total + inbox[h, s].astype(F32)
        return total

    def reduce_drain(part, inbox, r):
        for e in range(7):
            for h in range(2):
                reduce_edge(part, inbox, r, e, h)[0].wait_send()

    def reduce_leaves(part, inbox, r, term):
        term(at(2, 1))
        reduce_send(part, inbox, r, 0, 0)
        reduce_send(part, inbox, r, 0, 1)
        term(at(-1, 1))
        reduce_send(part, inbox, r, 1, 0)
        reduce_send(part, inbox, r, 2, 1)
        term(at(1, 1))
        reduce_send(part, inbox, r, 2, 0)
        reduce_send(part, inbox, r, 1, 1)
        term(at(1, 0))
        reduce_send(part, inbox, r, 3, 0)
        term(at(-1, 0))
        reduce_send(part, inbox, r, 3, 1)
        term(at(2, 0))
        term(at(0, 1))
        term(me)

    def grad_term(block):
        base = pl.multiple_of(block * width, width)

        @pl.loop(0, width // tile)
        def _(n):
            at_n = pl.multiple_of(n * tile, tile)
            row_n = pl.multiple_of(base + at_n, tile)
            term = dot(grad_val[...], wv[pl.ds(row_n, tile), :], NT)
            part_g[block, :, pl.ds(at_n, tile)] = term.astype(BF16)

    def grad_term_own(block):
        base = pl.multiple_of(block * width, width)

        @pl.loop(0, width // tile)
        def _(n):
            at_n = pl.multiple_of(n * tile, tile)
            row_n = pl.multiple_of(base + at_n, tile)
            term = dot(grad_val[...], wv[pl.ds(row_n, tile), :], NT)
            term = term + grad_q[:, pl.ds(at_n, tile)]
            part_g[block, :, pl.ds(at_n, tile)] = term.astype(BF16)

    def head_term(block):
        base = pl.multiple_of(block * width, width)

        @pl.loop(0, width // tile)
        def _(n):
            at_n = pl.multiple_of(n * tile, tile)
            col_n = pl.multiple_of(base + at_n, tile)
            term = dot(ctx[...], wo[:, pl.ds(col_n, tile)], NN)
            part_h[block, :, pl.ds(at_n, tile)] = term.astype(BF16)

    reduce_leaves(
        part_g, in_g, 0, lambda block: grad_term_own(block) if block is me else grad_term(block)
    )

    @pl.when(early)
    def _():
        gather_relay(rows_f, 2, 3, (4,))
        gather_wait(rows_f, 2, (1,))
        consume_rows(rows_f, near, first=True)

    reduce_relay(part_g, in_g, 0, 4, (0,))
    reduce_relay(part_g, in_g, 0, 6, (1, 2))

    @pl.when(early)
    def _():
        gather_wait(rows_f, 2, (4, 5, 6))
        consume_rows(rows_f, remote_blocks)
        val_f[...] = acc[...].astype(BF16)

    @pl.when(jnp.logical_not(early))
    def _():
        val_f[...] = val_b[...]

    reduce_relay(part_g, in_g, 0, 5, (4,))

    @pl.loop(0, heads)
    def _(head):
        cols = pl.ds(pl.multiple_of(head * HD, HD), HD)
        v = val_f[:, cols]
        low = probabilities(rows_f[me, :, cols], v).astype(BF16)
        ctx[:, cols] = dot(low, v, NN).astype(BF16)

    reduce_leaves(part_h, in_h, 1, head_term)

    for h in range(2):
        at_h = pl.ds(h * half, half)
        acc[at_h, :] = reduce_final(part_g, in_g, 0, h)
    grads = acc[...]
    unit = normed[...]
    gg_ref[...] = jnp.sum(grads * unit, axis=0, keepdims=True)
    grad_unit = grads * gain
    for step in range(1, PEERS):
        stat_copy(0, step).wait_send()
    row_sums(grad_unit, 0)
    row_sums(grad_unit * unit, 1)
    stats_send(1)
    reduce_relay(part_h, in_h, 1, 4, (0,))
    reduce_relay(part_h, in_h, 1, 6, (1, 2))
    means = stats_total(1)
    dx = cots[me].astype(F32) + inv_col[:, 0:1] * (
        acc[...] * gain - means[:, 0:1] - normed[...] * means[:, 1:2]
    )
    dx_buf[...] = dx.astype(BF16)
    send_dx = remote(dx_buf, ret_ref, far_send.at[1], far_recv.at[1], prev_section)
    send_dx.start()
    reduce_relay(part_h, in_h, 1, 5, (4,))
    send_y = []
    for h in range(2):
        at_h = pl.ds(h * half, half)
        y_buf[at_h, :] = (arr[at_h, :].astype(F32) + reduce_final(part_h, in_h, 1, h)).astype(BF16)
        copy = remote(
            y_buf.at[at_h], fwd_ref.at[at_h], far_send.at[2 + h], far_recv.at[2 + h], next_section
        )
        copy.start()
        send_y.append(copy)

    gather_drain(cots, 0)
    gather_drain(rows_b, 1)

    @pl.when(early)
    def _():
        gather_drain(rows_f, 2)

    reduce_drain(part_g, in_g, 0)
    reduce_drain(part_h, in_h, 1)
    for step in range(1, PEERS):
        stat_copy(1, step).wait_send()
    send_far.wait_send()
    keep_fet.wait()
    send_dx.wait()
    for copy in send_y:
        copy.wait()


def body(arriving, cotangent, evicted, ln_gain, value_weight, out_weight, fetch_slot):
    sections = lax.axis_size("section")
    position = lax.axis_index("section")
    length, width = arriving.shape[1:]
    full = PEERS * width
    send_slot = fetch_slot[sections - 1 - position]
    outgoing = lax.dynamic_index_in_dim(evicted[0], send_slot, 0, keepdims=False)
    half = length // 2
    anywhere = pl.BlockSpec(memory_space=pl.ANY)
    in_vmem = pl.BlockSpec(memory_space=pltpu.VMEM)
    rows = jax.ShapeDtypeStruct((length, width), BF16)
    dma = pltpu.SemaphoreType.DMA
    forwarded, returned, fetched, gain_grad = pl.pallas_call(
        functools.partial(kernel, sections),
        out_shape=(rows, rows, rows, jax.ShapeDtypeStruct((1, width), F32)),
        in_specs=[anywhere, anywhere, anywhere, in_vmem, anywhere, anywhere],
        out_specs=(anywhere, anywhere, anywhere, in_vmem),
        scratch_shapes=[
            pltpu.VMEM((full, width), BF16),
            pltpu.VMEM((width, full), BF16),
            pltpu.VMEM((PEERS, length, width), BF16),
            pltpu.VMEM((PEERS, length, width), BF16),
            pltpu.VMEM((PEERS, length, width), BF16),
            pltpu.VMEM((PEERS, length, width), BF16),
            pltpu.VMEM((PEERS, length, width), BF16),
            pltpu.VMEM((2, 7, half, width), BF16),
            pltpu.VMEM((2, 7, half, width), BF16),
            pltpu.VMEM((length, width), F32),
            pltpu.VMEM((length, width), BF16),
            pltpu.VMEM((length, width), BF16),
            pltpu.VMEM((length, width), BF16),
            pltpu.VMEM((length, width), BF16),
            pltpu.VMEM((length, width), F32),
            pltpu.VMEM((length, width), BF16),
            pltpu.VMEM((length, width), BF16),
            pltpu.VMEM((length, width), BF16),
            pltpu.VMEM((length, width), F32),
            pltpu.VMEM((length, HD), F32),
            pltpu.VMEM((8, length), F32),
            pltpu.VMEM((2, PEERS - 1, 8, length), F32),
            pltpu.VMEM((length, width), BF16),
            pltpu.VMEM((length, width), BF16),
            dma((5,)),
            dma((3, 2, 7)),
            dma((3, 2, 7)),
            dma((2, 2, 7)),
            dma((2, 2, 7)),
            dma((2, PEERS - 1)),
            dma((2, PEERS - 1)),
            dma((4,)),
            dma((4,)),
        ],
        compiler_params=pltpu.CompilerParams(
            collective_id=0, has_side_effects=True, vmem_limit_bytes=60 * 1024 * 1024
        ),
    )(arriving[0], cotangent[0], outgoing, ln_gain, value_weight[0], out_weight[0])
    return (forwarded[None], returned[None], gain_grad, fetched[None])


def solution(mesh):
    return jax.shard_map(
        body,
        mesh=mesh,
        in_specs=(
            P("section", None, "tp"),
            P("section", None, "tp"),
            P("section", None, None, "tp"),
            P("section", None),
            P("section", None, "tp"),
            P("section", "tp", None),
            P(),
        ),
        out_specs=(
            P("section", None, "tp"),
            P("section", None, "tp"),
            P("section", "tp"),
            P("section", None, "tp"),
        ),
        check_vma=False,
    )
```

```python
import functools
import math

import jax
import jax.numpy as jnp
from jax import lax
from jax.experimental import pallas as pl
from jax.experimental.pallas import tpu as pltpu
from jax.sharding import PartitionSpec as P

HD = 128
EPS = 1e-05
RING = 4
PEERS = 8
MESH = pl.DeviceIdType.MESH
BF16 = jnp.bfloat16
F32 = jnp.float32
NT = (((1,), (1,)), ((), ()))
NN = (((1,), (0,)), ((), ()))
TN = (((0,), (0,)), ((), ()))
OWNER = (0, 0)
TREE_X = (
    (OWNER, (1, 0)),
    (OWNER, (-1, 0)),
    (OWNER, (0, 1)),
    ((1, 0), (2, 0)),
    ((2, 0), (2, 1)),
    ((0, 1), (1, 1)),
    ((0, 1), (-1, 1)),
)
TREE_Z = (
    (OWNER, (1, 0)),
    (OWNER, (-1, 0)),
    (OWNER, (0, 1)),
    ((1, 0), (2, 0)),
    ((1, 0), (1, 1)),
    ((2, 0), (2, 1)),
    ((0, 1), (-1, 1)),
)
EDGES = len(TREE_X)
BLOCKS = (OWNER, (-1, 0), (1, 0), (0, 1), (2, 0), (-1, 1), (1, 1), (2, 1))


def children(tree, node):
    return [e for e, (a, _) in enumerate(tree) if a == node]


def depth(tree, e):
    a = tree[e][0]
    return 1 if a == OWNER else 1 + max(depth(tree, k) for k, (_, b) in enumerate(tree) if b == a)


def height(tree, e):
    below = children(tree, tree[e][1])
    return 1 + max(height(tree, k) for k in below) if below else 0


def two_chunks(first, count):
    half = count // 2
    return ((TREE_X, 1, first, half), (TREE_X, -1, first + half, half))


def three_chunks(count):
    side = max(16, count * 5 // 16 // 16 * 16)
    return (
        (TREE_X, 1, 0, side),
        (TREE_X, -1, side, side),
        (TREE_Z, 1, 2 * side, count - 2 * side),
    )


def dot(a, b, dims):
    return lax.dot_general(a, b, dims, preferred_element_type=F32)


def kernel(
    sections,
    arr_ref,
    cot_ref,
    ev_ref,
    slot_ref,
    gain_ref,
    wv_ref,
    wo_ref,
    fwd_ref,
    ret_ref,
    fet_ref,
    gg_ref,
    wv,
    wo,
    cots,
    rows_b,
    rows_f,
    part_g,
    part_h,
    in_g,
    in_h,
    acc,
    grad_ctx,
    val_b,
    val_f,
    grad_val,
    grad_q,
    ctx,
    arr,
    stored,
    outgoing,
    fet,
    far_rows,
    query,
    normed,
    inv_col,
    stat_out,
    stat_in,
    totals,
    far_totals,
    y_buf,
    dx_buf,
    loc_sem,
    ag_send,
    ag_recv,
    rs_send,
    rs_recv,
    st_send,
    st_recv,
    far_send,
    far_recv,
    help_send,
    help_recv,
):
    length, width = arr.shape
    half = length // 2
    helped = half
    chunks = two_chunks(0, length)
    whole = three_chunks(length)
    tables = (whole, whole, two_chunks(helped, length - helped), two_chunks(0, helped))
    heads = width // HD
    full = PEERS * width
    tile = min(256, width)
    section = lax.axis_index("section")
    rank = lax.axis_index("tp")
    x = rank % RING
    z = rank // RING
    early = section < sections // 2
    late = section >= sections // 2

    def at(dx, dz):
        return lax.rem(z + dz, 2) * RING + lax.rem(x + dx + RING, RING)

    def peer(dx, dz):
        return (section, at(dx, dz))

    def remote(src, dst, ssem, rsem, device):
        return pltpu.make_async_remote_copy(
            src_ref=src,
            dst_ref=dst,
            send_sem=ssem,
            recv_sem=rsem,
            device_id=device,
            device_id_type=MESH,
        )

    me = at(0, 0)
    next_section = (lax.rem(section + 1, sections), rank)
    prev_section = (lax.rem(section + sections - 1, sections), rank)
    mirror = (sections - 1 - section, rank)
    helper = (sections - 1 - section, at(0, 1))

    load_cot = pltpu.make_async_copy(cot_ref, cots.at[me], loc_sem.at[0])
    load_arr = pltpu.make_async_copy(arr_ref, arr, loc_sem.at[1])
    load_wo = pltpu.make_async_copy(wo_ref, wo, loc_sem.at[2])
    load_wv = pltpu.make_async_copy(wv_ref, wv, loc_sem.at[3])
    load_evicted = pltpu.make_async_copy(ev_ref, stored, loc_sem.at[5])
    load_evicted.start()
    load_cot.start()
    load_arr.start()

    barrier = pltpu.get_barrier_semaphore()
    for step in range(1, PEERS):
        pl.semaphore_signal(
            barrier, inc=1, device_id=(section, lax.rem(rank + step, PEERS)), device_id_type=MESH
        )
    for device in (next_section, prev_section, mirror, helper):
        pl.semaphore_signal(barrier, inc=1, device_id=device, device_id_type=MESH)
    pl.semaphore_wait(barrier, PEERS + 3)

    def gather_edge(buf, g, c, e, landing=False):
        tree, p, first, count = tables[g][c]
        a, b = tree[e]
        dx, dz = b if landing else a
        rows = buf.at[at(-dx * p, dz), pl.ds(first, count)]
        device = peer((b[0] - a[0]) * p, (b[1] - a[1]) % 2)
        return remote(rows, rows, ag_send.at[g, c, e], ag_recv.at[g, c, e], device)

    def gather_roots(buf, g):
        for e in range(3):
            for c in range(len(tables[g])):
                gather_edge(buf, g, c, e).start()

    def gather_relay(buf, g, level):
        for e in (0, 2, 1, 3, 4, 5, 6):
            for c, (tree, *_) in enumerate(tables[g]):
                onward = children(tree, tree[e][1])
                if depth(tree, e) == level and onward:
                    gather_edge(buf, g, c, e, True).wait_recv()
                    for o in onward:
                        gather_edge(buf, g, c, o).start()

    def gather_wait(buf, g, near_only):
        for e in range(EDGES):
            for c, (tree, *_) in enumerate(tables[g]):
                leaf = not children(tree, tree[e][1])
                if leaf and (depth(tree, e) == 1) == near_only:
                    gather_edge(buf, g, c, e, True).wait_recv()

    def gather_drain(buf, g):
        for e in range(EDGES):
            for c in range(len(tables[g])):
                gather_edge(buf, g, c, e).wait_send()

    def help_copy(j, landing=False):
        dx, dz = BLOCKS[j]
        block = at(dx, (dz + 1) % 2) if landing else at(dx, dz)
        return remote(
            rows_b.at[block, pl.ds(0, helped)],
            far_rows.at[block],
            help_send.at[j],
            help_recv.at[j],
            helper,
        )

    def consume_cot(blocks, first=False):
        for block in blocks:
            base = pl.multiple_of(block * width, width)

            @pl.loop(0, width // tile)
            def _(n):
                at_n = pl.multiple_of(n * tile, tile)
                term = dot(cots[block], wo[pl.ds(at_n, tile), pl.ds(base, width)], NT)
                if first:
                    acc[:, pl.ds(at_n, tile)] = term
                else:
                    acc[:, pl.ds(at_n, tile)] += term

            first = False

    def consume_rows(buf, blocks, first=False):
        for block in blocks:
            base = pl.multiple_of(block * width, width)

            @pl.loop(0, width // tile)
            def _(n):
                at_n = pl.multiple_of(n * tile, tile)
                term = dot(buf[block], wv[pl.ds(base, width), pl.ds(at_n, tile)], NN)
                if first:
                    acc[:, pl.ds(at_n, tile)] = term
                else:
                    acc[:, pl.ds(at_n, tile)] += term

            first = False

    blocks = [at(*rel) for rel in BLOCKS]
    near, remote_blocks = blocks[:4], blocks[4:]

    def row_sums(values, turn, row):
        total = values[:, 0:HD]
        for c in range(1, heads):
            total = total + values[:, c * HD : (c + 1) * HD]
        sums = jnp.sum(total.T, axis=0, keepdims=True)
        stat_out[turn, pl.ds(row, 1), pl.ds(0, values.shape[0])] = sums

    def stat_copy(turn, step):
        device = (section, lax.rem(rank + step, PEERS))
        return remote(
            stat_out.at[turn],
            stat_in.at[turn, step - 1],
            st_send.at[turn, step - 1],
            st_recv.at[turn, step - 1],
            device,
        )

    def stats_send(turn):
        for step in range(1, PEERS):
            stat_copy(turn, step).start()

    def stats_total(turn):
        total = stat_out[turn]
        for step in range(1, PEERS):
            stat_copy(turn, step).wait_recv()
            total = total + stat_in[turn, step - 1]
        return total / full

    row_at = lax.broadcasted_iota(jnp.int32, (length, length), 0)
    col_at = lax.broadcasted_iota(jnp.int32, (length, length), 1)
    scale = 1.0 / math.sqrt(HD)

    def probabilities(q, v):
        scores = dot(q, v, NT) * scale
        scores = jnp.where(col_at <= row_at, scores, -jnp.inf)
        top = jnp.max(scores, axis=-1, keepdims=True)
        e = jnp.exp(scores - top)
        return e / jnp.sum(e, axis=-1, keepdims=True)

    def reduce_edge(part, inbox, r, c, e):
        tree, p, first, count = chunks[c]
        a, b = tree[e]
        return remote(
            part.at[at(-b[0] * p, b[1]), pl.ds(first, count)],
            inbox.at[e, pl.ds(first, count)],
            rs_send.at[r, c, e],
            rs_recv.at[r, c, e],
            peer((a[0] - b[0]) * p, (a[1] - b[1]) % 2),
        )

    def reduce_leaves(part, inbox, r, term):
        for block in ((2, 1), (-1, 1), (1, 1), (1, 0), (-1, 0), (2, 0), (0, 1), OWNER):
            term(block)
            for c, (tree, p, *_) in enumerate(chunks):
                for e, (_, b) in enumerate(tree):
                    same = ((-b[0] * p) % RING, b[1]) == (block[0] % RING, block[1])
                    if same and height(tree, e) == 0:
                        reduce_edge(part, inbox, r, c, e).start()

    def reduce_relay(part, inbox, r, level):
        for e in (3, 2, 1, 0, 4, 5, 6):
            for c, (tree, p, first, count) in enumerate(chunks):
                if height(tree, e) != level:
                    continue
                b = tree[e][1]
                block, rows = at(-b[0] * p, b[1]), pl.ds(first, count)
                total = part[block, rows].astype(F32)
                for k in children(tree, b):
                    reduce_edge(part, inbox, r, c, k).wait_recv()
                    total = total + inbox[k, rows].astype(F32)
                part[block, rows] = total.astype(BF16)
                reduce_edge(part, inbox, r, c, e).start()

    def reduce_final(part, inbox, r, c):
        _, _, first, count = chunks[c]
        rows = pl.ds(first, count)
        total = part[me, rows].astype(F32)
        for k in (1, 2, 0):
            reduce_edge(part, inbox, r, c, k).wait_recv()
            total = total + inbox[k, rows].astype(F32)
        return rows, total

    def reduce_drain(part, inbox, r):
        for e in range(EDGES):
            for c in range(len(chunks)):
                reduce_edge(part, inbox, r, c, e).wait_send()

    def grad_term(rel):
        block = at(*rel)
        base = pl.multiple_of(block * width, width)

        @pl.loop(0, width // tile)
        def _(n):
            at_n = pl.multiple_of(n * tile, tile)
            row_n = pl.multiple_of(base + at_n, tile)
            term = dot(grad_val[...], wv[pl.ds(row_n, tile), :], NT)
            if rel == OWNER:
                term = term + grad_q[:, pl.ds(at_n, tile)]
            part_g[block, :, pl.ds(at_n, tile)] = term.astype(BF16)

    def head_term(rel):
        block = at(*rel)
        base = pl.multiple_of(block * width, width)

        @pl.loop(0, width // tile)
        def _(n):
            at_n = pl.multiple_of(n * tile, tile)
            col_n = pl.multiple_of(base + at_n, tile)
            term = dot(ctx[...], wo[:, pl.ds(col_n, tile)], NN)
            part_h[block, :, pl.ds(at_n, tile)] = term.astype(BF16)

    gain = gain_ref[:, pl.ds(pl.multiple_of(rank * width, width), width)]
    top, bottom = pl.ds(0, helped), pl.ds(helped, length - helped)

    def normalise(values, centre, inv, rows):
        unit = (values.astype(F32) - centre) * inv
        normed[rows, :] = unit
        inv_col[rows, :] = jnp.broadcast_to(inv, (unit.shape[0], HD))
        return (unit * gain).astype(BF16)

    def centre_and_inv(means):
        centre = means[:, 0:1]
        return centre, lax.rsqrt(means[:, 1:2] - centre * centre + EPS)

    def send_totals():
        return remote(totals, far_totals, far_send.at[6], far_recv.at[6], mirror)

    def far_half(k, rows):
        return remote(outgoing.at[rows], fet.at[rows], far_send.at[k], far_recv.at[k], mirror)

    def helped_rows():
        for j in range(PEERS):
            help_copy(j, True).wait_recv()
        pltpu.make_async_copy(far_rows.at[me], fet_ref.at[top], loc_sem.at[5]).start()
        total = jnp.zeros((helped, HD), F32)
        squares = jnp.zeros((helped, HD), F32)
        for block in range(PEERS):
            for c in range(heads):
                part = far_rows[block, :, c * HD : (c + 1) * HD].astype(F32)
                total = total + part
                squares = squares + part * part
        centre = jnp.sum(total, axis=-1, keepdims=True) / full
        square = jnp.sum(squares, axis=-1, keepdims=True) / full
        inv = lax.rsqrt(square - centre * centre + EPS)
        for block in range(PEERS):
            unit = (far_rows[block].astype(F32) - centre) * inv
            gain_block = gain_ref[:, block * width : (block + 1) * width]
            rows_b[block, top] = (unit * gain_block).astype(BF16)
        normalise(far_rows[me], centre, inv, top)

    load_evicted.wait()
    outgoing[...] = jnp.where(slot_ref[sections - 1 - section] == 0, stored[0], stored[1])

    @pl.when(late)
    def _():
        rows_b[me, top] = outgoing[top, :]
        gather_roots(rows_b, 3)
        help_copy(0).start()

    load_arr.wait()
    stat_out[...] = jnp.zeros_like(stat_out)
    own = arr[...].astype(F32)
    row_sums(own, 0, 0)
    row_sums(own * own, 0, 1)
    away = outgoing[...].astype(F32)
    row_sums(away, 0, 2)
    row_sums(away * away, 0, 3)
    stats_send(0)
    load_cot.wait()

    @pl.when(early)
    def _():
        gather_roots(cots, 0)

    load_wv.start()
    load_wo.start()

    @pl.when(late)
    def _():
        gather_relay(rows_b, 3, 1)
        gather_wait(rows_b, 3, True)
        for j in range(1, 4):
            help_copy(j).start()
        gather_relay(rows_b, 3, 2)

    means = stats_total(0)
    totals[...] = means
    rows_f[me] = normalise(arr[...], *centre_and_inv(means.T), pl.ds(0, length))
    gather_roots(rows_f, 1)
    send_totals().start()
    far_half(0, bottom).start()
    gather_relay(rows_f, 1, 1)
    send_totals().wait_recv()
    far_half(0, bottom).wait_recv()
    keep_bottom = pltpu.make_async_copy(fet.at[bottom], fet_ref.at[bottom], loc_sem.at[4])
    keep_bottom.start()

    @pl.when(early)
    def _():
        far_means = far_totals[...].T[helped:, 2:4]
        rows_b[me, bottom] = normalise(fet[bottom, :], *centre_and_inv(far_means), bottom)

    @pl.when(late)
    def _():
        gather_roots(cots, 0)
        gather_wait(rows_b, 3, False)
        for j in range(4, 8):
            help_copy(j).start()

    gather_relay(rows_f, 1, 2)

    @pl.when(early)
    def _():
        gather_roots(rows_b, 2)
        far_half(1, top).start()

    load_wv.wait()
    gather_wait(rows_f, 1, True)
    consume_rows(rows_f, near, first=True)
    gather_relay(cots, 0, 1)

    @pl.when(early)
    def _():
        gather_relay(rows_b, 2, 1)

    gather_wait(rows_f, 1, False)
    consume_rows(rows_f, remote_blocks)
    val_f[...] = acc[...].astype(BF16)
    load_wo.wait()
    gather_wait(cots, 0, True)
    consume_cot(near, first=True)
    gather_relay(cots, 0, 2)

    @pl.loop(0, heads)
    def _(head):
        cols = pl.ds(pl.multiple_of(head * HD, HD), HD)
        v = val_f[:, cols]
        low = probabilities(rows_f[me, :, cols], v).astype(BF16)
        ctx[:, cols] = dot(low, v, NN).astype(BF16)

    @pl.when(early)
    def _():
        gather_relay(rows_b, 2, 2)

    reduce_leaves(part_h, in_h, 0, head_term)

    @pl.when(early)
    def _():
        helped_rows()

    gather_wait(cots, 0, False)
    consume_cot(remote_blocks)
    grad_ctx[...] = acc[...].astype(BF16)

    @pl.when(early)
    def _():
        gather_wait(rows_b, 2, True)
        gather_wait(rows_b, 2, False)
        consume_rows(rows_b, blocks, first=True)
        val_b[...] = acc[...].astype(BF16)
        query[...] = rows_b[me]

    @pl.when(late)
    def _():
        far_half(1, top).wait_recv()
        pltpu.make_async_copy(fet.at[top], fet_ref.at[top], loc_sem.at[5]).start()
        val_b[...] = val_f[...]
        query[...] = rows_f[me]

    @pl.loop(0, heads)
    def _(head):
        cols = pl.ds(pl.multiple_of(head * HD, HD), HD)
        q = query[:, cols]
        v = val_b[:, cols]
        g = grad_ctx[:, cols]
        probs = probabilities(q, v)
        low = probs.astype(BF16)
        grad_probs = dot(g, v, NT)
        inner = jnp.sum(grad_probs * probs, axis=-1, keepdims=True)
        grad_low = (probs * (grad_probs - inner) * scale).astype(BF16)
        grad_val[:, cols] = (dot(low, g, TN) + dot(grad_low, q, TN)).astype(BF16)
        grad_q[:, cols] = dot(grad_low, v, NN)

    reduce_leaves(part_g, in_g, 1, grad_term)

    def gradient_sums(scaled):
        first = jnp.zeros((length, HD), F32)
        second = jnp.zeros((length, HD), F32)
        for block in range(PEERS):
            for c in range(heads):
                cols = slice(c * HD, (c + 1) * HD)
                term = part_g[block, :, cols].astype(F32)
                gain_cols = slice(block * width + c * HD, block * width + (c + 1) * HD)
                first = first + term * gain_ref[:, gain_cols]
                second = second + term * scaled[block, :, cols].astype(F32)
        stat_out[1, 0:1, :] = jnp.sum(first.T, axis=0, keepdims=True)
        stat_out[1, 1:2, :] = jnp.sum(second.T, axis=0, keepdims=True)

    @pl.when(early)
    def _():
        gradient_sums(rows_b)

    @pl.when(late)
    def _():
        gradient_sums(rows_f)

    stats_send(1)
    reduce_relay(part_g, in_g, 1, 1)
    reduce_relay(part_h, in_h, 0, 1)
    reduce_relay(part_g, in_g, 1, 2)
    reduce_relay(part_h, in_h, 0, 2)
    means = stats_total(1).T
    gain_sum = jnp.zeros((1, width), F32)
    shifts = []
    for c in range(len(chunks)):
        rows, grads = reduce_final(part_g, in_g, 1, c)
        unit = normed[rows, :]
        dx = cots[me, rows].astype(F32) + inv_col[rows, 0:1] * (
            grads * gain
            - means[c * half : (c + 1) * half, 0:1]
            - unit * means[c * half : (c + 1) * half, 1:2]
        )
        dx_buf[rows, :] = dx.astype(BF16)
        copy = remote(
            dx_buf.at[rows], ret_ref.at[rows], far_send.at[2 + c], far_recv.at[2 + c], prev_section
        )
        copy.start()
        shifts.append(copy)
        gain_sum = gain_sum + jnp.sum(grads * unit, axis=0, keepdims=True)
    for c in range(len(chunks)):
        rows, total = reduce_final(part_h, in_h, 0, c)
        y_buf[rows, :] = (arr[rows, :].astype(F32) + total).astype(BF16)
        copy = remote(
            y_buf.at[rows], fwd_ref.at[rows], far_send.at[4 + c], far_recv.at[4 + c], next_section
        )
        copy.start()
        shifts.append(copy)
    gg_ref[...] = gain_sum

    gather_drain(cots, 0)
    gather_drain(rows_f, 1)
    for step in range(1, PEERS):
        stat_copy(0, step).wait_send()
        stat_copy(1, step).wait_send()

    @pl.when(early)
    def _():
        gather_drain(rows_b, 2)
        far_half(1, top).wait_send()
        pltpu.make_async_copy(far_rows.at[me], fet_ref.at[top], loc_sem.at[5]).wait()

    @pl.when(late)
    def _():
        gather_drain(rows_b, 3)
        for j in range(PEERS):
            help_copy(j).wait_send()
        pltpu.make_async_copy(fet.at[top], fet_ref.at[top], loc_sem.at[5]).wait()

    reduce_drain(part_g, in_g, 1)
    reduce_drain(part_h, in_h, 0)
    far_half(0, bottom).wait_send()
    keep_bottom.wait()
    send_totals().wait_send()
    for copy in shifts:
        copy.wait()


def publish(*refs):
    landed, results, held, sems = refs[:4], refs[4:8], refs[8:12], refs[12]
    inward = [pltpu.make_async_copy(landed[i], held[i], sems.at[0, i]) for i in range(4)]
    outward = [pltpu.make_async_copy(held[i], results[i], sems.at[1, i]) for i in range(4)]
    for copy in inward:
        copy.start()
    for i in range(4):
        inward[i].wait()
        outward[i].start()
    for copy in outward:
        copy.wait()


def body(arriving, cotangent, evicted, ln_gain, value_weight, out_weight, fetch_slot):
    sections = lax.axis_size("section")
    length, width = arriving.shape[1:]
    full = PEERS * width
    anywhere = pl.BlockSpec(memory_space=pl.ANY)
    in_vmem = pl.BlockSpec(memory_space=pltpu.VMEM)
    in_smem = pl.BlockSpec(memory_space=pltpu.SMEM)
    rows = jax.ShapeDtypeStruct((length, width), BF16)
    dma = pltpu.SemaphoreType.DMA
    gathered = pltpu.VMEM((PEERS, length, width), BF16)
    inbox = pltpu.VMEM((EDGES, length, width), BF16)
    share = pltpu.VMEM((length, width), BF16)
    wide = pltpu.VMEM((length, width), F32)
    out_shape = (rows, rows, rows, jax.ShapeDtypeStruct((1, width), F32))
    landed = pl.pallas_call(
        functools.partial(kernel, sections),
        out_shape=out_shape,
        in_specs=[anywhere, anywhere, anywhere, in_smem, in_vmem, anywhere, anywhere],
        out_specs=(anywhere, anywhere, anywhere, in_vmem),
        scratch_shapes=[
            pltpu.VMEM((full, width), BF16),
            pltpu.VMEM((width, full), BF16),
            gathered,
            gathered,
            gathered,
            gathered,
            gathered,
            inbox,
            inbox,
            wide,
            share,
            share,
            share,
            share,
            wide,
            share,
            share,
            pltpu.VMEM((2, length, width), BF16),
            share,
            share,
            pltpu.VMEM((PEERS, length // 2, width), BF16),
            share,
            wide,
            pltpu.VMEM((length, HD), F32),
            pltpu.VMEM((2, 8, length), F32),
            pltpu.VMEM((2, PEERS - 1, 8, length), F32),
            pltpu.VMEM((8, length), F32),
            pltpu.VMEM((8, length), F32),
            share,
            share,
            dma((6,)),
            dma((4, 3, EDGES)),
            dma((4, 3, EDGES)),
            dma((2, 2, EDGES)),
            dma((2, 2, EDGES)),
            dma((2, PEERS - 1)),
            dma((2, PEERS - 1)),
            dma((7,)),
            dma((7,)),
            dma((PEERS,)),
            dma((PEERS,)),
        ],
        compiler_params=pltpu.CompilerParams(
            collective_id=0, has_side_effects=True, vmem_limit_bytes=60 * 1024 * 1024
        ),
    )(arriving[0], cotangent[0], evicted[0], fetch_slot, ln_gain, value_weight[0], out_weight[0])
    forwarded, returned, fetched, gain_grad = pl.pallas_call(
        publish,
        out_shape=out_shape,
        in_specs=[anywhere] * 4,
        out_specs=(anywhere,) * 4,
        scratch_shapes=[share, share, share, pltpu.VMEM((1, width), F32), dma((2, 4))],
        compiler_params=pltpu.CompilerParams(vmem_limit_bytes=60 * 1024 * 1024),
    )(*landed)
    return (forwarded[None], returned[None], gain_grad, fetched[None])


def solution(mesh):
    return jax.shard_map(
        body,
        mesh=mesh,
        in_specs=(
            P("section", None, "tp"),
            P("section", None, "tp"),
            P("section", None, None, "tp"),
            P("section", None),
            P("section", None, "tp"),
            P("section", "tp", None),
            P(),
        ),
        out_specs=(
            P("section", None, "tp"),
            P("section", None, "tp"),
            P("section", "tp"),
            P("section", None, "tp"),
        ),
        check_vma=False,
    )
```

```python
import functools
import math

import jax
import jax.numpy as jnp
from jax import lax
from jax.experimental import pallas as pl
from jax.experimental.pallas import tpu as pltpu
from jax.sharding import PartitionSpec as P

HD = 128
EPS = 1e-05
RING = 4
PEERS = 8
MESH = pl.DeviceIdType.MESH
BF16 = jnp.bfloat16
F32 = jnp.float32
NT = (((1,), (1,)), ((), ()))
NN = (((1,), (0,)), ((), ()))
TN = (((0,), (0,)), ((), ()))
OWNER = (0, 0)
TREE_X = (
    (OWNER, (1, 0)),
    (OWNER, (-1, 0)),
    (OWNER, (0, 1)),
    ((1, 0), (2, 0)),
    ((2, 0), (2, 1)),
    ((0, 1), (1, 1)),
    ((0, 1), (-1, 1)),
)
TREE_Z = (
    (OWNER, (1, 0)),
    (OWNER, (-1, 0)),
    (OWNER, (0, 1)),
    ((1, 0), (2, 0)),
    ((1, 0), (1, 1)),
    ((2, 0), (2, 1)),
    ((0, 1), (-1, 1)),
)
EDGES = len(TREE_X)
BLOCKS = (OWNER, (-1, 0), (1, 0), (0, 1), (2, 0), (-1, 1), (1, 1), (2, 1))


def children(tree, node):
    return [e for e, (a, _) in enumerate(tree) if a == node]


def depth(tree, e):
    a = tree[e][0]
    return 1 if a == OWNER else 1 + max(depth(tree, k) for k, (_, b) in enumerate(tree) if b == a)


def height(tree, e):
    below = children(tree, tree[e][1])
    return 1 + max(height(tree, k) for k in below) if below else 0


def two_chunks(first, count):
    half = count // 2
    return ((TREE_X, 1, first, half), (TREE_X, -1, first + half, half))


def three_chunks(count):
    side = max(16, count * 5 // 16 // 16 * 16)
    return (
        (TREE_X, 1, 0, side),
        (TREE_X, -1, side, side),
        (TREE_Z, 1, 2 * side, count - 2 * side),
    )


def dot(a, b, dims):
    return lax.dot_general(a, b, dims, preferred_element_type=F32)


def kernel(
    sections,
    arr_ref,
    cot_ref,
    ev_ref,
    slot_ref,
    gain_ref,
    wv_ref,
    wo_ref,
    fwd_ref,
    ret_ref,
    fet_ref,
    gg_ref,
    wv,
    wo,
    cots,
    rows_b,
    rows_f,
    part_g,
    part_h,
    in_g,
    in_h,
    acc,
    grad_ctx,
    val_b,
    val_f,
    grad_val,
    grad_q,
    ctx,
    arr,
    stored,
    outgoing,
    fet,
    far_rows,
    query,
    normed,
    inv_col,
    stat_out,
    stat_in,
    totals,
    far_totals,
    y_buf,
    dx_buf,
    loc_sem,
    ag_send,
    ag_recv,
    rs_send,
    rs_recv,
    st_send,
    st_recv,
    far_send,
    far_recv,
    help_send,
    help_recv,
):
    length, width = arr.shape
    half = length // 2
    helped = half
    chunks = two_chunks(0, length)
    whole = three_chunks(length)
    tables = (whole, whole, two_chunks(helped, length - helped), two_chunks(0, helped))
    heads = width // HD
    full = PEERS * width
    section = lax.axis_index("section")
    rank = lax.axis_index("tp")
    x = rank % RING
    z = rank // RING
    early = section < sections // 2
    late = section >= sections // 2

    def at(dx, dz):
        return lax.rem(z + dz, 2) * RING + lax.rem(x + dx + RING, RING)

    def peer(dx, dz):
        return (section, at(dx, dz))

    def remote(src, dst, ssem, rsem, device):
        return pltpu.make_async_remote_copy(
            src_ref=src,
            dst_ref=dst,
            send_sem=ssem,
            recv_sem=rsem,
            device_id=device,
            device_id_type=MESH,
        )

    me = at(0, 0)
    next_section = (lax.rem(section + 1, sections), rank)
    prev_section = (lax.rem(section + sections - 1, sections), rank)
    mirror = (sections - 1 - section, rank)
    helper = (sections - 1 - section, at(0, 1))

    load_cot = pltpu.make_async_copy(cot_ref, cots.at[me], loc_sem.at[0])
    load_arr = pltpu.make_async_copy(arr_ref, arr, loc_sem.at[1])
    load_wo = pltpu.make_async_copy(wo_ref, wo, loc_sem.at[2])
    load_wv = pltpu.make_async_copy(wv_ref, wv, loc_sem.at[3])
    load_evicted = pltpu.make_async_copy(ev_ref, stored, loc_sem.at[5])
    load_evicted.start()
    load_cot.start()
    load_arr.start()

    barrier = pltpu.get_barrier_semaphore()
    for step in range(1, PEERS):
        pl.semaphore_signal(
            barrier, inc=1, device_id=(section, lax.rem(rank + step, PEERS)), device_id_type=MESH
        )
    for device in (next_section, prev_section, mirror, helper):
        pl.semaphore_signal(barrier, inc=1, device_id=device, device_id_type=MESH)
    pl.semaphore_wait(barrier, PEERS + 3)

    def gather_edge(buf, g, c, e, landing=False):
        tree, p, first, count = tables[g][c]
        a, b = tree[e]
        dx, dz = b if landing else a
        rows = buf.at[at(-dx * p, dz), pl.ds(first, count)]
        device = peer((b[0] - a[0]) * p, (b[1] - a[1]) % 2)
        return remote(rows, rows, ag_send.at[g, c, e], ag_recv.at[g, c, e], device)

    def gather_roots(buf, g):
        for e in range(3):
            for c in range(len(tables[g])):
                gather_edge(buf, g, c, e).start()

    def gather_relay(buf, g, level):
        for e in (0, 2, 1, 3, 4, 5, 6):
            for c, (tree, *_) in enumerate(tables[g]):
                onward = children(tree, tree[e][1])
                if depth(tree, e) == level and onward:
                    gather_edge(buf, g, c, e, True).wait_recv()
                    for o in onward:
                        gather_edge(buf, g, c, o).start()

    def gather_wait(buf, g, near_only):
        for e in range(EDGES):
            for c, (tree, *_) in enumerate(tables[g]):
                leaf = not children(tree, tree[e][1])
                if leaf and (depth(tree, e) == 1) == near_only:
                    gather_edge(buf, g, c, e, True).wait_recv()

    def gather_drain(buf, g):
        for e in range(EDGES):
            for c in range(len(tables[g])):
                gather_edge(buf, g, c, e).wait_send()

    def help_copy(j, landing=False):
        dx, dz = BLOCKS[j]
        block = at(dx, (dz + 1) % 2) if landing else at(dx, dz)
        return remote(
            rows_b.at[block, pl.ds(0, helped)],
            far_rows.at[block],
            help_send.at[j],
            help_recv.at[j],
            helper,
        )

    def consume_cot(blocks, first=False):
        for block in blocks:
            base = pl.multiple_of(block * width, width)
            term = dot(cots[block], wo[:, pl.ds(base, width)], NT)
            acc[...] = term if first else acc[...] + term
            first = False

    def consume_rows(buf, blocks, first=False):
        for block in blocks:
            base = pl.multiple_of(block * width, width)
            term = dot(buf[block], wv[pl.ds(base, width), :], NN)
            acc[...] = term if first else acc[...] + term
            first = False

    blocks = [at(*rel) for rel in BLOCKS]
    near, remote_blocks = blocks[:4], blocks[4:]

    def row_sums(values, turn, row):
        total = values[:, 0:HD]
        for c in range(1, heads):
            total = total + values[:, c * HD : (c + 1) * HD]
        sums = jnp.sum(total.T, axis=0, keepdims=True)
        stat_out[turn, pl.ds(row, 1), pl.ds(0, values.shape[0])] = sums

    def stat_copy(turn, step):
        device = (section, lax.rem(rank + step, PEERS))
        return remote(
            stat_out.at[turn],
            stat_in.at[turn, step - 1],
            st_send.at[turn, step - 1],
            st_recv.at[turn, step - 1],
            device,
        )

    def stats_send(turn):
        for step in range(1, PEERS):
            stat_copy(turn, step).start()

    def stats_total(turn):
        total = stat_out[turn]
        for step in range(1, PEERS):
            stat_copy(turn, step).wait_recv()
            total = total + stat_in[turn, step - 1]
        return total / full

    row_at = lax.broadcasted_iota(jnp.int32, (length, length), 0)
    col_at = lax.broadcasted_iota(jnp.int32, (length, length), 1)
    scale = 1.0 / math.sqrt(HD)

    def probabilities(q, v):
        scores = dot(q, v, NT) * scale
        scores = jnp.where(col_at <= row_at, scores, -jnp.inf)
        top = jnp.max(scores, axis=-1, keepdims=True)
        e = jnp.exp(scores - top)
        return e / jnp.sum(e, axis=-1, keepdims=True)

    def reduce_edge(part, inbox, r, c, e):
        tree, p, first, count = chunks[c]
        a, b = tree[e]
        return remote(
            part.at[at(-b[0] * p, b[1]), pl.ds(first, count)],
            inbox.at[e, pl.ds(first, count)],
            rs_send.at[r, c, e],
            rs_recv.at[r, c, e],
            peer((a[0] - b[0]) * p, (a[1] - b[1]) % 2),
        )

    def reduce_leaves(part, inbox, r, term):
        for block in ((2, 1), (-1, 1), (1, 1), (1, 0), (-1, 0), (2, 0), (0, 1), OWNER):
            term(block)
            for c, (tree, p, *_) in enumerate(chunks):
                for e, (_, b) in enumerate(tree):
                    same = ((-b[0] * p) % RING, b[1]) == (block[0] % RING, block[1])
                    if same and height(tree, e) == 0:
                        reduce_edge(part, inbox, r, c, e).start()

    def reduce_relay(part, inbox, r, level):
        for e in (3, 2, 1, 0, 4, 5, 6):
            for c, (tree, p, first, count) in enumerate(chunks):
                if height(tree, e) != level:
                    continue
                b = tree[e][1]
                block, rows = at(-b[0] * p, b[1]), pl.ds(first, count)
                total = part[block, rows].astype(F32)
                for k in children(tree, b):
                    reduce_edge(part, inbox, r, c, k).wait_recv()
                    total = total + inbox[k, rows].astype(F32)
                part[block, rows] = total.astype(BF16)
                reduce_edge(part, inbox, r, c, e).start()

    def reduce_final(part, inbox, r, c):
        _, _, first, count = chunks[c]
        rows = pl.ds(first, count)
        total = part[me, rows].astype(F32)
        for k in (1, 2, 0):
            reduce_edge(part, inbox, r, c, k).wait_recv()
            total = total + inbox[k, rows].astype(F32)
        return rows, total

    def reduce_drain(part, inbox, r):
        for e in range(EDGES):
            for c in range(len(chunks)):
                reduce_edge(part, inbox, r, c, e).wait_send()

    def grad_term(rel):
        block = at(*rel)
        base = pl.multiple_of(block * width, width)
        term = dot(grad_val[...], wv[pl.ds(base, width), :], NT)
        if rel == OWNER:
            term = term + grad_q[...]
        part_g[block] = term.astype(BF16)

    def head_term(rel):
        block = at(*rel)
        base = pl.multiple_of(block * width, width)
        part_h[block] = dot(ctx[...], wo[:, pl.ds(base, width)], NN).astype(BF16)

    gain = gain_ref[:, pl.ds(pl.multiple_of(rank * width, width), width)]
    top, bottom = pl.ds(0, helped), pl.ds(helped, length - helped)

    def normalise(values, centre, inv, rows):
        unit = (values.astype(F32) - centre) * inv
        normed[rows, :] = unit
        inv_col[rows, :] = jnp.broadcast_to(inv, (unit.shape[0], HD))
        return (unit * gain).astype(BF16)

    def centre_and_inv(means):
        centre = means[:, 0:1]
        return centre, lax.rsqrt(means[:, 1:2] - centre * centre + EPS)

    def send_totals():
        return remote(totals, far_totals, far_send.at[6], far_recv.at[6], mirror)

    def far_half(k, rows):
        return remote(outgoing.at[rows], fet.at[rows], far_send.at[k], far_recv.at[k], mirror)

    def helped_rows():
        for j in range(PEERS):
            help_copy(j, True).wait_recv()
        pltpu.make_async_copy(far_rows.at[me], fet_ref.at[top], loc_sem.at[5]).start()
        total = jnp.zeros((helped, HD), F32)
        squares = jnp.zeros((helped, HD), F32)
        for block in range(PEERS):
            for c in range(heads):
                part = far_rows[block, :, c * HD : (c + 1) * HD].astype(F32)
                total = total + part
                squares = squares + part * part
        centre = jnp.sum(total, axis=-1, keepdims=True) / full
        square = jnp.sum(squares, axis=-1, keepdims=True) / full
        inv = lax.rsqrt(square - centre * centre + EPS)
        for block in range(PEERS):
            unit = (far_rows[block].astype(F32) - centre) * inv
            gain_block = gain_ref[:, block * width : (block + 1) * width]
            rows_b[block, top] = (unit * gain_block).astype(BF16)
        normalise(far_rows[me], centre, inv, top)

    load_evicted.wait()
    outgoing[...] = jnp.where(slot_ref[sections - 1 - section] == 0, stored[0], stored[1])

    @pl.when(late)
    def _():
        rows_b[me, top] = outgoing[top, :]
        gather_roots(rows_b, 3)
        help_copy(0).start()

    load_arr.wait()
    stat_out[...] = jnp.zeros_like(stat_out)
    own = arr[...].astype(F32)
    row_sums(own, 0, 0)
    row_sums(own * own, 0, 1)
    away = outgoing[...].astype(F32)
    row_sums(away, 0, 2)
    row_sums(away * away, 0, 3)
    stats_send(0)
    load_cot.wait()

    @pl.when(early)
    def _():
        gather_roots(cots, 0)

    load_wv.start()
    load_wo.start()

    @pl.when(late)
    def _():
        gather_relay(rows_b, 3, 1)
        gather_wait(rows_b, 3, True)
        for j in range(1, 4):
            help_copy(j).start()
        gather_relay(rows_b, 3, 2)

    means = stats_total(0)
    totals[...] = means
    rows_f[me] = normalise(arr[...], *centre_and_inv(means.T), pl.ds(0, length))
    gather_roots(rows_f, 1)
    send_totals().start()
    far_half(0, bottom).start()
    gather_relay(rows_f, 1, 1)
    send_totals().wait_recv()
    far_half(0, bottom).wait_recv()
    keep_bottom = pltpu.make_async_copy(fet.at[bottom], fet_ref.at[bottom], loc_sem.at[4])
    keep_bottom.start()

    @pl.when(early)
    def _():
        far_means = far_totals[...].T[helped:, 2:4]
        rows_b[me, bottom] = normalise(fet[bottom, :], *centre_and_inv(far_means), bottom)

    @pl.when(late)
    def _():
        gather_roots(cots, 0)
        gather_wait(rows_b, 3, False)
        for j in range(4, 8):
            help_copy(j).start()

    gather_relay(rows_f, 1, 2)

    @pl.when(early)
    def _():
        gather_roots(rows_b, 2)
        far_half(1, top).start()

    load_wv.wait()
    gather_wait(rows_f, 1, True)
    consume_rows(rows_f, near, first=True)
    gather_relay(cots, 0, 1)

    @pl.when(early)
    def _():
        gather_relay(rows_b, 2, 1)

    gather_wait(rows_f, 1, False)
    consume_rows(rows_f, remote_blocks)
    val_f[...] = acc[...].astype(BF16)
    load_wo.wait()
    gather_wait(cots, 0, True)
    consume_cot(near, first=True)
    gather_relay(cots, 0, 2)

    for head in range(heads):
        cols = pl.ds(head * HD, HD)
        v = val_f[:, cols]
        low = probabilities(rows_f[me, :, cols], v).astype(BF16)
        ctx[:, cols] = dot(low, v, NN).astype(BF16)

    @pl.when(early)
    def _():
        gather_relay(rows_b, 2, 2)

    reduce_leaves(part_h, in_h, 0, head_term)

    @pl.when(early)
    def _():
        helped_rows()

    gather_wait(cots, 0, False)
    consume_cot(remote_blocks)
    grad_ctx[...] = acc[...].astype(BF16)

    @pl.when(early)
    def _():
        gather_wait(rows_b, 2, True)
        gather_wait(rows_b, 2, False)
        consume_rows(rows_b, blocks, first=True)
        val_b[...] = acc[...].astype(BF16)
        query[...] = rows_b[me]

    @pl.when(late)
    def _():
        far_half(1, top).wait_recv()
        pltpu.make_async_copy(fet.at[top], fet_ref.at[top], loc_sem.at[5]).start()
        val_b[...] = val_f[...]
        query[...] = rows_f[me]

    for head in range(heads):
        cols = pl.ds(head * HD, HD)
        q = query[:, cols]
        v = val_b[:, cols]
        g = grad_ctx[:, cols]
        probs = probabilities(q, v)
        low = probs.astype(BF16)
        grad_probs = dot(g, v, NT)
        inner = jnp.sum(grad_probs * probs, axis=-1, keepdims=True)
        grad_low = (probs * (grad_probs - inner) * scale).astype(BF16)
        grad_val[:, cols] = (dot(low, g, TN) + dot(grad_low, q, TN)).astype(BF16)
        grad_q[:, cols] = dot(grad_low, v, NN)

    reduce_leaves(part_g, in_g, 1, grad_term)

    def gradient_sums(scaled):
        first = jnp.zeros((length, HD), F32)
        second = jnp.zeros((length, HD), F32)
        for block in range(PEERS):
            for c in range(heads):
                cols = slice(c * HD, (c + 1) * HD)
                term = part_g[block, :, cols].astype(F32)
                gain_cols = slice(block * width + c * HD, block * width + (c + 1) * HD)
                first = first + term * gain_ref[:, gain_cols]
                second = second + term * scaled[block, :, cols].astype(F32)
        stat_out[1, 0:1, :] = jnp.sum(first.T, axis=0, keepdims=True)
        stat_out[1, 1:2, :] = jnp.sum(second.T, axis=0, keepdims=True)

    @pl.when(early)
    def _():
        gradient_sums(rows_b)

    @pl.when(late)
    def _():
        gradient_sums(rows_f)

    stats_send(1)
    reduce_relay(part_g, in_g, 1, 1)
    reduce_relay(part_h, in_h, 0, 1)
    reduce_relay(part_g, in_g, 1, 2)
    reduce_relay(part_h, in_h, 0, 2)
    means = stats_total(1).T
    gain_sum = jnp.zeros((1, width), F32)
    shifts = []
    for c in range(len(chunks)):
        rows, grads = reduce_final(part_g, in_g, 1, c)
        unit = normed[rows, :]
        dx = cots[me, rows].astype(F32) + inv_col[rows, 0:1] * (
            grads * gain
            - means[c * half : (c + 1) * half, 0:1]
            - unit * means[c * half : (c + 1) * half, 1:2]
        )
        dx_buf[rows, :] = dx.astype(BF16)
        copy = remote(
            dx_buf.at[rows], ret_ref.at[rows], far_send.at[2 + c], far_recv.at[2 + c], prev_section
        )
        copy.start()
        shifts.append(copy)
        gain_sum = gain_sum + jnp.sum(grads * unit, axis=0, keepdims=True)
    for c in range(len(chunks)):
        rows, total = reduce_final(part_h, in_h, 0, c)
        y_buf[rows, :] = (arr[rows, :].astype(F32) + total).astype(BF16)
        copy = remote(
            y_buf.at[rows], fwd_ref.at[rows], far_send.at[4 + c], far_recv.at[4 + c], next_section
        )
        copy.start()
        shifts.append(copy)
    gg_ref[...] = gain_sum

    gather_drain(cots, 0)
    gather_drain(rows_f, 1)
    for step in range(1, PEERS):
        stat_copy(0, step).wait_send()
        stat_copy(1, step).wait_send()

    @pl.when(early)
    def _():
        gather_drain(rows_b, 2)
        far_half(1, top).wait_send()
        pltpu.make_async_copy(far_rows.at[me], fet_ref.at[top], loc_sem.at[5]).wait()

    @pl.when(late)
    def _():
        gather_drain(rows_b, 3)
        for j in range(PEERS):
            help_copy(j).wait_send()
        pltpu.make_async_copy(fet.at[top], fet_ref.at[top], loc_sem.at[5]).wait()

    reduce_drain(part_g, in_g, 1)
    reduce_drain(part_h, in_h, 0)
    far_half(0, bottom).wait_send()
    keep_bottom.wait()
    send_totals().wait_send()
    for copy in shifts:
        copy.wait()


def publish(*refs):
    landed, results, held, sems = refs[:4], refs[4:8], refs[8:12], refs[12]
    inward = [pltpu.make_async_copy(landed[i], held[i], sems.at[0, i]) for i in range(4)]
    outward = [pltpu.make_async_copy(held[i], results[i], sems.at[1, i]) for i in range(4)]
    for copy in inward:
        copy.start()
    for i in range(4):
        inward[i].wait()
        outward[i].start()
    for copy in outward:
        copy.wait()


def body(arriving, cotangent, evicted, ln_gain, value_weight, out_weight, fetch_slot):
    sections = lax.axis_size("section")
    length, width = arriving.shape[1:]
    full = PEERS * width
    anywhere = pl.BlockSpec(memory_space=pl.ANY)
    in_vmem = pl.BlockSpec(memory_space=pltpu.VMEM)
    in_smem = pl.BlockSpec(memory_space=pltpu.SMEM)
    rows = jax.ShapeDtypeStruct((length, width), BF16)
    dma = pltpu.SemaphoreType.DMA
    gathered = pltpu.VMEM((PEERS, length, width), BF16)
    inbox = pltpu.VMEM((EDGES, length, width), BF16)
    share = pltpu.VMEM((length, width), BF16)
    wide = pltpu.VMEM((length, width), F32)
    out_shape = (rows, rows, rows, jax.ShapeDtypeStruct((1, width), F32))
    landed = pl.pallas_call(
        functools.partial(kernel, sections),
        out_shape=out_shape,
        in_specs=[anywhere, anywhere, anywhere, in_smem, in_vmem, anywhere, anywhere],
        out_specs=(anywhere, anywhere, anywhere, in_vmem),
        scratch_shapes=[
            pltpu.VMEM((full, width), BF16),
            pltpu.VMEM((width, full), BF16),
            gathered,
            gathered,
            gathered,
            gathered,
            gathered,
            inbox,
            inbox,
            wide,
            share,
            share,
            share,
            share,
            wide,
            share,
            share,
            pltpu.VMEM((2, length, width), BF16),
            share,
            share,
            pltpu.VMEM((PEERS, length // 2, width), BF16),
            share,
            wide,
            pltpu.VMEM((length, HD), F32),
            pltpu.VMEM((2, 8, length), F32),
            pltpu.VMEM((2, PEERS - 1, 8, length), F32),
            pltpu.VMEM((8, length), F32),
            pltpu.VMEM((8, length), F32),
            share,
            share,
            dma((6,)),
            dma((4, 3, EDGES)),
            dma((4, 3, EDGES)),
            dma((2, 2, EDGES)),
            dma((2, 2, EDGES)),
            dma((2, PEERS - 1)),
            dma((2, PEERS - 1)),
            dma((7,)),
            dma((7,)),
            dma((PEERS,)),
            dma((PEERS,)),
        ],
        compiler_params=pltpu.CompilerParams(
            collective_id=0, has_side_effects=True, vmem_limit_bytes=60 * 1024 * 1024
        ),
    )(arriving[0], cotangent[0], evicted[0], fetch_slot, ln_gain, value_weight[0], out_weight[0])
    forwarded, returned, fetched, gain_grad = pl.pallas_call(
        publish,
        out_shape=out_shape,
        in_specs=[anywhere] * 4,
        out_specs=(anywhere,) * 4,
        scratch_shapes=[share, share, share, pltpu.VMEM((1, width), F32), dma((2, 4))],
        compiler_params=pltpu.CompilerParams(vmem_limit_bytes=60 * 1024 * 1024),
    )(*landed)
    return (forwarded[None], returned[None], gain_grad, fetched[None])


def solution(mesh):
    return jax.shard_map(
        body,
        mesh=mesh,
        in_specs=(
            P("section", None, "tp"),
            P("section", None, "tp"),
            P("section", None, None, "tp"),
            P("section", None),
            P("section", None, "tp"),
            P("section", "tp", None),
            P(),
        ),
        out_specs=(
            P("section", None, "tp"),
            P("section", None, "tp"),
            P("section", "tp"),
            P("section", None, "tp"),
        ),
        check_vma=False,
    )
```

```python
import functools
import math

import jax
import jax.numpy as jnp
from jax import lax
from jax.experimental import pallas as pl
from jax.experimental.pallas import tpu as pltpu
from jax.sharding import PartitionSpec as P

HD = 128
EPS = 1e-05
RING = 4
PEERS = 8
MESH = pl.DeviceIdType.MESH
BF16 = jnp.bfloat16
F32 = jnp.float32
NT = (((1,), (1,)), ((), ()))
NN = (((1,), (0,)), ((), ()))
TN = (((0,), (0,)), ((), ()))
OWNER = (0, 0)
TREE_X = (
    (OWNER, (1, 0)),
    (OWNER, (-1, 0)),
    (OWNER, (0, 1)),
    ((1, 0), (2, 0)),
    ((2, 0), (2, 1)),
    ((0, 1), (1, 1)),
    ((0, 1), (-1, 1)),
)
TREE_Z = (
    (OWNER, (1, 0)),
    (OWNER, (-1, 0)),
    (OWNER, (0, 1)),
    ((1, 0), (2, 0)),
    ((1, 0), (1, 1)),
    ((2, 0), (2, 1)),
    ((0, 1), (-1, 1)),
)
EDGES = len(TREE_X)
BLOCKS = (OWNER, (-1, 0), (1, 0), (0, 1), (2, 0), (-1, 1), (1, 1), (2, 1))


def children(tree, node):
    return [e for e, (a, _) in enumerate(tree) if a == node]


def depth(tree, e):
    a = tree[e][0]
    return 1 if a == OWNER else 1 + max(depth(tree, k) for k, (_, b) in enumerate(tree) if b == a)


def height(tree, e):
    below = children(tree, tree[e][1])
    return 1 + max(height(tree, k) for k in below) if below else 0


def two_chunks(first, count):
    half = count // 2
    return ((TREE_X, 1, first, half), (TREE_X, -1, first + half, half))


def three_chunks(count):
    side = max(16, count * 5 // 16 // 16 * 16)
    return (
        (TREE_X, 1, 0, side),
        (TREE_X, -1, side, side),
        (TREE_Z, 1, 2 * side, count - 2 * side),
    )


def dot(a, b, dims):
    return lax.dot_general(a, b, dims, preferred_element_type=F32)


def kernel(
    sections,
    arr_ref,
    cot_ref,
    ev_ref,
    slot_ref,
    gain_ref,
    wv_ref,
    wo_ref,
    fwd_ref,
    ret_ref,
    fet_ref,
    gg_ref,
    wv,
    wo,
    cots,
    rows_b,
    rows_f,
    part_g,
    part_h,
    in_g,
    in_h,
    acc,
    grad_ctx,
    val_b,
    val_f,
    grad_val,
    grad_q,
    ctx,
    arr,
    stored,
    outgoing,
    fet,
    far_rows,
    query,
    normed,
    inv_col,
    stat_out,
    stat_in,
    totals,
    far_totals,
    y_buf,
    dx_buf,
    loc_sem,
    ag_send,
    ag_recv,
    rs_send,
    rs_recv,
    st_send,
    st_recv,
    far_send,
    far_recv,
    help_send,
    help_recv,
):
    length, width = arr.shape
    half = length // 2
    helped = length * 3 // 8
    chunks = two_chunks(0, length)
    whole = three_chunks(length)
    tables = (whole, whole, two_chunks(helped, length - helped), two_chunks(0, helped))
    heads = width // HD
    full = PEERS * width
    section = lax.axis_index("section")
    rank = lax.axis_index("tp")
    x = rank % RING
    z = rank // RING
    early = section < sections // 2
    late = section >= sections // 2

    def at(dx, dz):
        return lax.rem(z + dz, 2) * RING + lax.rem(x + dx + RING, RING)

    def peer(dx, dz):
        return (section, at(dx, dz))

    def remote(src, dst, ssem, rsem, device):
        return pltpu.make_async_remote_copy(
            src_ref=src,
            dst_ref=dst,
            send_sem=ssem,
            recv_sem=rsem,
            device_id=device,
            device_id_type=MESH,
        )

    me = at(0, 0)
    next_section = (lax.rem(section + 1, sections), rank)
    prev_section = (lax.rem(section + sections - 1, sections), rank)
    mirror = (sections - 1 - section, rank)
    helper = (sections - 1 - section, at(0, 1))

    load_cot = pltpu.make_async_copy(cot_ref, cots.at[me], loc_sem.at[0])
    load_arr = pltpu.make_async_copy(arr_ref, arr, loc_sem.at[1])
    load_wo = pltpu.make_async_copy(wo_ref, wo, loc_sem.at[2])
    load_wv = pltpu.make_async_copy(wv_ref, wv, loc_sem.at[3])
    load_evicted = pltpu.make_async_copy(ev_ref, stored, loc_sem.at[5])
    load_evicted.start()
    load_cot.start()
    load_arr.start()

    barrier = pltpu.get_barrier_semaphore()
    for step in range(1, PEERS):
        pl.semaphore_signal(
            barrier, inc=1, device_id=(section, lax.rem(rank + step, PEERS)), device_id_type=MESH
        )
    for device in (next_section, prev_section, mirror, helper):
        pl.semaphore_signal(barrier, inc=1, device_id=device, device_id_type=MESH)
    pl.semaphore_wait(barrier, PEERS + 3)

    def gather_edge(buf, g, c, e, landing=False):
        tree, p, first, count = tables[g][c]
        a, b = tree[e]
        dx, dz = b if landing else a
        rows = buf.at[at(-dx * p, dz), pl.ds(first, count)]
        device = peer((b[0] - a[0]) * p, (b[1] - a[1]) % 2)
        return remote(rows, rows, ag_send.at[g, c, e], ag_recv.at[g, c, e], device)

    def gather_roots(buf, g):
        for e in range(3):
            for c in range(len(tables[g])):
                gather_edge(buf, g, c, e).start()

    def gather_relay(buf, g, level):
        for e in (0, 2, 1, 3, 4, 5, 6):
            for c, (tree, *_) in enumerate(tables[g]):
                onward = children(tree, tree[e][1])
                if depth(tree, e) == level and onward:
                    gather_edge(buf, g, c, e, True).wait_recv()
                    for o in onward:
                        gather_edge(buf, g, c, o).start()

    def gather_wait(buf, g, near_only):
        for e in range(EDGES):
            for c, (tree, *_) in enumerate(tables[g]):
                leaf = not children(tree, tree[e][1])
                if leaf and (depth(tree, e) == 1) == near_only:
                    gather_edge(buf, g, c, e, True).wait_recv()

    def gather_drain(buf, g):
        for e in range(EDGES):
            for c in range(len(tables[g])):
                gather_edge(buf, g, c, e).wait_send()

    def help_copy(j, landing=False):
        dx, dz = BLOCKS[j]
        block = at(dx, (dz + 1) % 2) if landing else at(dx, dz)
        return remote(
            rows_b.at[block, pl.ds(0, helped)],
            far_rows.at[block],
            help_send.at[j],
            help_recv.at[j],
            helper,
        )

    def consume_cot(blocks, first=False):
        for block in blocks:
            base = pl.multiple_of(block * width, width)
            term = dot(cots[block], wo[:, pl.ds(base, width)], NT)
            acc[...] = term if first else acc[...] + term
            first = False

    def consume_rows(buf, blocks, first=False):
        for block in blocks:
            base = pl.multiple_of(block * width, width)
            term = dot(buf[block], wv[pl.ds(base, width), :], NN)
            acc[...] = term if first else acc[...] + term
            first = False

    blocks = [at(*rel) for rel in BLOCKS]
    near, remote_blocks = blocks[:4], blocks[4:]

    def row_sums(values, turn, row):
        total = values[:, 0:HD]
        for c in range(1, heads):
            total = total + values[:, c * HD : (c + 1) * HD]
        sums = jnp.sum(total.T, axis=0, keepdims=True)
        stat_out[turn, pl.ds(row, 1), pl.ds(0, values.shape[0])] = sums

    def stat_copy(turn, step):
        device = (section, lax.rem(rank + step, PEERS))
        return remote(
            stat_out.at[turn],
            stat_in.at[turn, step - 1],
            st_send.at[turn, step - 1],
            st_recv.at[turn, step - 1],
            device,
        )

    def stats_send(turn):
        for step in range(1, PEERS):
            stat_copy(turn, step).start()

    def stats_total(turn):
        total = stat_out[turn]
        for step in range(1, PEERS):
            stat_copy(turn, step).wait_recv()
            total = total + stat_in[turn, step - 1]
        return total / full

    row_at = lax.broadcasted_iota(jnp.int32, (length, length), 0)
    col_at = lax.broadcasted_iota(jnp.int32, (length, length), 1)
    scale = 1.0 / math.sqrt(HD)

    def probabilities(q, v):
        scores = dot(q, v, NT) * scale
        scores = jnp.where(col_at <= row_at, scores, -jnp.inf)
        top = jnp.max(scores, axis=-1, keepdims=True)
        e = jnp.exp(scores - top)
        return e / jnp.sum(e, axis=-1, keepdims=True)

    def reduce_edge(part, inbox, r, c, e):
        tree, p, first, count = chunks[c]
        a, b = tree[e]
        return remote(
            part.at[at(-b[0] * p, b[1]), pl.ds(first, count)],
            inbox.at[e, pl.ds(first, count)],
            rs_send.at[r, c, e],
            rs_recv.at[r, c, e],
            peer((a[0] - b[0]) * p, (a[1] - b[1]) % 2),
        )

    def reduce_leaves(part, inbox, r, term):
        for block in ((2, 1), (-1, 1), (1, 1), (1, 0), (-1, 0), (2, 0), (0, 1), OWNER):
            term(block)
            for c, (tree, p, *_) in enumerate(chunks):
                for e, (_, b) in enumerate(tree):
                    same = ((-b[0] * p) % RING, b[1]) == (block[0] % RING, block[1])
                    if same and height(tree, e) == 0:
                        reduce_edge(part, inbox, r, c, e).start()

    def reduce_relay(part, inbox, r, level):
        for e in (3, 2, 1, 0, 4, 5, 6):
            for c, (tree, p, first, count) in enumerate(chunks):
                if height(tree, e) != level:
                    continue
                b = tree[e][1]
                block, rows = at(-b[0] * p, b[1]), pl.ds(first, count)
                total = part[block, rows].astype(F32)
                for k in children(tree, b):
                    reduce_edge(part, inbox, r, c, k).wait_recv()
                    total = total + inbox[k, rows].astype(F32)
                part[block, rows] = total.astype(BF16)
                reduce_edge(part, inbox, r, c, e).start()

    def reduce_final(part, inbox, r, c):
        _, _, first, count = chunks[c]
        rows = pl.ds(first, count)
        total = part[me, rows].astype(F32)
        for k in (1, 2, 0):
            reduce_edge(part, inbox, r, c, k).wait_recv()
            total = total + inbox[k, rows].astype(F32)
        return rows, total

    def reduce_drain(part, inbox, r):
        for e in range(EDGES):
            for c in range(len(chunks)):
                reduce_edge(part, inbox, r, c, e).wait_send()

    def grad_term(rel):
        block = at(*rel)
        base = pl.multiple_of(block * width, width)
        term = dot(grad_val[...], wv[pl.ds(base, width), :], NT)
        if rel == OWNER:
            term = term + grad_q[...]
        part_g[block] = term.astype(BF16)

    def head_term(rel):
        block = at(*rel)
        base = pl.multiple_of(block * width, width)
        part_h[block] = dot(ctx[...], wo[:, pl.ds(base, width)], NN).astype(BF16)

    gain = gain_ref[:, pl.ds(pl.multiple_of(rank * width, width), width)]
    top, bottom = pl.ds(0, helped), pl.ds(helped, length - helped)

    def normalise(values, centre, inv, rows):
        unit = (values.astype(F32) - centre) * inv
        normed[rows, :] = unit
        inv_col[rows, :] = jnp.broadcast_to(inv, (unit.shape[0], HD))
        return (unit * gain).astype(BF16)

    def centre_and_inv(means):
        centre = means[:, 0:1]
        return centre, lax.rsqrt(means[:, 1:2] - centre * centre + EPS)

    def send_totals():
        return remote(totals, far_totals, far_send.at[6], far_recv.at[6], mirror)

    def far_half(k, rows):
        return remote(outgoing.at[rows], fet.at[rows], far_send.at[k], far_recv.at[k], mirror)

    def helped_rows():
        for j in range(PEERS):
            help_copy(j, True).wait_recv()
        pltpu.make_async_copy(far_rows.at[me], fet_ref.at[top], loc_sem.at[5]).start()
        total = jnp.zeros((helped, HD), F32)
        squares = jnp.zeros((helped, HD), F32)
        for block in range(PEERS):
            for c in range(heads):
                part = far_rows[block, :, c * HD : (c + 1) * HD].astype(F32)
                total = total + part
                squares = squares + part * part
        centre = jnp.sum(total, axis=-1, keepdims=True) / full
        square = jnp.sum(squares, axis=-1, keepdims=True) / full
        inv = lax.rsqrt(square - centre * centre + EPS)
        for block in range(PEERS):
            unit = (far_rows[block].astype(F32) - centre) * inv
            gain_block = gain_ref[:, block * width : (block + 1) * width]
            rows_b[block, top] = (unit * gain_block).astype(BF16)
        normalise(far_rows[me], centre, inv, top)

    load_evicted.wait()
    outgoing[...] = jnp.where(slot_ref[sections - 1 - section] == 0, stored[0], stored[1])

    @pl.when(late)
    def _():
        rows_b[me, top] = outgoing[top, :]
        gather_roots(rows_b, 3)
        help_copy(0).start()

    load_arr.wait()
    stat_out[...] = jnp.zeros_like(stat_out)
    own = arr[...].astype(F32)
    row_sums(own, 0, 0)
    row_sums(own * own, 0, 1)
    away = outgoing[...].astype(F32)
    row_sums(away, 0, 2)
    row_sums(away * away, 0, 3)
    stats_send(0)
    load_cot.wait()

    @pl.when(early)
    def _():
        gather_roots(cots, 0)

    load_wv.start()
    load_wo.start()

    @pl.when(late)
    def _():
        gather_relay(rows_b, 3, 1)
        gather_wait(rows_b, 3, True)
        for j in range(1, 4):
            help_copy(j).start()
        gather_relay(rows_b, 3, 2)

    means = stats_total(0)
    totals[...] = means
    rows_f[me] = normalise(arr[...], *centre_and_inv(means.T), pl.ds(0, length))
    gather_roots(rows_f, 1)
    send_totals().start()
    far_half(0, bottom).start()
    gather_relay(rows_f, 1, 1)
    send_totals().wait_recv()
    far_half(0, bottom).wait_recv()
    keep_bottom = pltpu.make_async_copy(fet.at[bottom], fet_ref.at[bottom], loc_sem.at[4])
    keep_bottom.start()

    @pl.when(early)
    def _():
        far_means = far_totals[...].T[helped:, 2:4]
        rows_b[me, bottom] = normalise(fet[bottom, :], *centre_and_inv(far_means), bottom)

    @pl.when(late)
    def _():
        gather_roots(cots, 0)
        gather_wait(rows_b, 3, False)
        for j in range(4, 8):
            help_copy(j).start()

    gather_relay(rows_f, 1, 2)

    @pl.when(early)
    def _():
        gather_roots(rows_b, 2)
        far_half(1, top).start()

    load_wv.wait()
    gather_wait(rows_f, 1, True)
    consume_rows(rows_f, near, first=True)
    gather_relay(cots, 0, 1)

    @pl.when(early)
    def _():
        gather_relay(rows_b, 2, 1)

    gather_wait(rows_f, 1, False)
    consume_rows(rows_f, remote_blocks)
    val_f[...] = acc[...].astype(BF16)
    load_wo.wait()
    gather_wait(cots, 0, True)
    consume_cot(near, first=True)
    gather_relay(cots, 0, 2)

    for head in range(heads):
        cols = pl.ds(head * HD, HD)
        v = val_f[:, cols]
        low = probabilities(rows_f[me, :, cols], v).astype(BF16)
        ctx[:, cols] = dot(low, v, NN).astype(BF16)

    @pl.when(early)
    def _():
        gather_relay(rows_b, 2, 2)

    reduce_leaves(part_h, in_h, 0, head_term)

    @pl.when(early)
    def _():
        helped_rows()

    gather_wait(cots, 0, False)
    consume_cot(remote_blocks)
    grad_ctx[...] = acc[...].astype(BF16)

    @pl.when(early)
    def _():
        gather_wait(rows_b, 2, True)
        gather_wait(rows_b, 2, False)
        consume_rows(rows_b, blocks, first=True)
        val_b[...] = acc[...].astype(BF16)
        query[...] = rows_b[me]

    @pl.when(late)
    def _():
        far_half(1, top).wait_recv()
        pltpu.make_async_copy(fet.at[top], fet_ref.at[top], loc_sem.at[5]).start()
        val_b[...] = val_f[...]
        query[...] = rows_f[me]

    for head in range(heads):
        cols = pl.ds(head * HD, HD)
        q = query[:, cols]
        v = val_b[:, cols]
        g = grad_ctx[:, cols]
        probs = probabilities(q, v)
        low = probs.astype(BF16)
        grad_probs = dot(g, v, NT)
        inner = jnp.sum(grad_probs * probs, axis=-1, keepdims=True)
        grad_low = (probs * (grad_probs - inner) * scale).astype(BF16)
        grad_val[:, cols] = (dot(low, g, TN) + dot(grad_low, q, TN)).astype(BF16)
        grad_q[:, cols] = dot(grad_low, v, NN)

    reduce_leaves(part_g, in_g, 1, grad_term)

    def gradient_sums(scaled):
        first = jnp.zeros((length, HD), F32)
        second = jnp.zeros((length, HD), F32)
        for block in range(PEERS):
            for c in range(heads):
                cols = slice(c * HD, (c + 1) * HD)
                term = part_g[block, :, cols].astype(F32)
                gain_cols = slice(block * width + c * HD, block * width + (c + 1) * HD)
                first = first + term * gain_ref[:, gain_cols]
                second = second + term * scaled[block, :, cols].astype(F32)
        stat_out[1, 0:1, :] = jnp.sum(first.T, axis=0, keepdims=True)
        stat_out[1, 1:2, :] = jnp.sum(second.T, axis=0, keepdims=True)

    @pl.when(early)
    def _():
        gradient_sums(rows_b)

    @pl.when(late)
    def _():
        gradient_sums(rows_f)

    stats_send(1)
    reduce_relay(part_g, in_g, 1, 1)
    reduce_relay(part_h, in_h, 0, 1)
    reduce_relay(part_g, in_g, 1, 2)
    reduce_relay(part_h, in_h, 0, 2)
    means = stats_total(1).T
    gain_sum = jnp.zeros((1, width), F32)
    shifts = []
    for c in range(len(chunks)):
        rows, grads = reduce_final(part_g, in_g, 1, c)
        unit = normed[rows, :]
        dx = cots[me, rows].astype(F32) + inv_col[rows, 0:1] * (
            grads * gain
            - means[c * half : (c + 1) * half, 0:1]
            - unit * means[c * half : (c + 1) * half, 1:2]
        )
        dx_buf[rows, :] = dx.astype(BF16)
        copy = remote(
            dx_buf.at[rows], ret_ref.at[rows], far_send.at[2 + c], far_recv.at[2 + c], prev_section
        )
        copy.start()
        shifts.append(copy)
        gain_sum = gain_sum + jnp.sum(grads * unit, axis=0, keepdims=True)
    for c in range(len(chunks)):
        rows, total = reduce_final(part_h, in_h, 0, c)
        y_buf[rows, :] = (arr[rows, :].astype(F32) + total).astype(BF16)
        copy = remote(
            y_buf.at[rows], fwd_ref.at[rows], far_send.at[4 + c], far_recv.at[4 + c], next_section
        )
        copy.start()
        shifts.append(copy)
    gg_ref[...] = gain_sum

    gather_drain(cots, 0)
    gather_drain(rows_f, 1)
    for step in range(1, PEERS):
        stat_copy(0, step).wait_send()
        stat_copy(1, step).wait_send()

    @pl.when(early)
    def _():
        gather_drain(rows_b, 2)
        far_half(1, top).wait_send()
        pltpu.make_async_copy(far_rows.at[me], fet_ref.at[top], loc_sem.at[5]).wait()

    @pl.when(late)
    def _():
        gather_drain(rows_b, 3)
        for j in range(PEERS):
            help_copy(j).wait_send()
        pltpu.make_async_copy(fet.at[top], fet_ref.at[top], loc_sem.at[5]).wait()

    reduce_drain(part_g, in_g, 1)
    reduce_drain(part_h, in_h, 0)
    far_half(0, bottom).wait_send()
    keep_bottom.wait()
    send_totals().wait_send()
    for copy in shifts:
        copy.wait()


def publish(*refs):
    landed, results, held, sems = refs[:4], refs[4:8], refs[8:12], refs[12]
    inward = [pltpu.make_async_copy(landed[i], held[i], sems.at[0, i]) for i in range(4)]
    outward = [pltpu.make_async_copy(held[i], results[i], sems.at[1, i]) for i in range(4)]
    for copy in inward:
        copy.start()
    for i in range(4):
        inward[i].wait()
        outward[i].start()
    for copy in outward:
        copy.wait()


def body(arriving, cotangent, evicted, ln_gain, value_weight, out_weight, fetch_slot):
    sections = lax.axis_size("section")
    length, width = arriving.shape[1:]
    full = PEERS * width
    anywhere = pl.BlockSpec(memory_space=pl.ANY)
    in_vmem = pl.BlockSpec(memory_space=pltpu.VMEM)
    in_smem = pl.BlockSpec(memory_space=pltpu.SMEM)
    rows = jax.ShapeDtypeStruct((length, width), BF16)
    dma = pltpu.SemaphoreType.DMA
    gathered = pltpu.VMEM((PEERS, length, width), BF16)
    inbox = pltpu.VMEM((EDGES, length, width), BF16)
    share = pltpu.VMEM((length, width), BF16)
    wide = pltpu.VMEM((length, width), F32)
    out_shape = (rows, rows, rows, jax.ShapeDtypeStruct((1, width), F32))
    landed = pl.pallas_call(
        functools.partial(kernel, sections),
        out_shape=out_shape,
        in_specs=[anywhere, anywhere, anywhere, in_smem, in_vmem, anywhere, anywhere],
        out_specs=(anywhere, anywhere, anywhere, in_vmem),
        scratch_shapes=[
            pltpu.VMEM((full, width), BF16),
            pltpu.VMEM((width, full), BF16),
            gathered,
            gathered,
            gathered,
            gathered,
            gathered,
            inbox,
            inbox,
            wide,
            share,
            share,
            share,
            share,
            wide,
            share,
            share,
            pltpu.VMEM((2, length, width), BF16),
            share,
            share,
            pltpu.VMEM((PEERS, length * 3 // 8, width), BF16),
            share,
            wide,
            pltpu.VMEM((length, HD), F32),
            pltpu.VMEM((2, 8, length), F32),
            pltpu.VMEM((2, PEERS - 1, 8, length), F32),
            pltpu.VMEM((8, length), F32),
            pltpu.VMEM((8, length), F32),
            share,
            share,
            dma((6,)),
            dma((4, 3, EDGES)),
            dma((4, 3, EDGES)),
            dma((2, 2, EDGES)),
            dma((2, 2, EDGES)),
            dma((2, PEERS - 1)),
            dma((2, PEERS - 1)),
            dma((7,)),
            dma((7,)),
            dma((PEERS,)),
            dma((PEERS,)),
        ],
        compiler_params=pltpu.CompilerParams(
            collective_id=0, has_side_effects=True, vmem_limit_bytes=60 * 1024 * 1024
        ),
    )(arriving[0], cotangent[0], evicted[0], fetch_slot, ln_gain, value_weight[0], out_weight[0])
    forwarded, returned, fetched, gain_grad = pl.pallas_call(
        publish,
        out_shape=out_shape,
        in_specs=[anywhere] * 4,
        out_specs=(anywhere,) * 4,
        scratch_shapes=[share, share, share, pltpu.VMEM((1, width), F32), dma((2, 4))],
        compiler_params=pltpu.CompilerParams(vmem_limit_bytes=60 * 1024 * 1024),
    )(*landed)
    return (forwarded[None], returned[None], gain_grad, fetched[None])


def solution(mesh):
    return jax.shard_map(
        body,
        mesh=mesh,
        in_specs=(
            P("section", None, "tp"),
            P("section", None, "tp"),
            P("section", None, None, "tp"),
            P("section", None),
            P("section", None, "tp"),
            P("section", "tp", None),
            P(),
        ),
        out_specs=(
            P("section", None, "tp"),
            P("section", None, "tp"),
            P("section", "tp"),
            P("section", None, "tp"),
        ),
        check_vma=False,
    )
```
